32 devices in a mesh: tm: 8 (over z, y), grp: 4 (over x, core).
Axes of the slice: x: 2, y: 2, z: 4, core: 2. Of those that a mesh axis runs over, the one named last changes fastest.
Arguments:
- voltages: bfloat16 [1, 24, 2, 2, 262144], P(None, None, None, None, ('tm', 'grp')), may hold values from -8 to 8
- chirp_phase: float32 [24, 512, 512], P(None, 'tm'), may hold values from -3.140625 to 3.140625
- intersection: int32 [24], replicated, may hold values from 1 to 131072
- group_of: int32 [24], replicated, may hold values from 0 to 3, as said below
Outputs:
- group_power: float32 [1, 4, 131072], P(None, None, ('tm', 'grp'))
The draws below stay inside these ranges and needn't reach their ends.
Inputs may be any that keep to these rules, and one draw needn't show every extreme that they name: `group_of`: every one of the 4 groups holds at least one channel and at most 12; some group holds exactly 12.
All inputs are finite; a program needn't handle non-finite values.
Results may differ from the reference program's by a relative error of at most 0.0003.
Values may be sent and summed in bfloat16 or wider, within the bound.
A program may use at most 128 MiB of HBM per device.

```python
import math
import jax
import jax.numpy as jnp
from jax import lax

BEAMS = 1
POLS = 2
CHANS = 24
NFFT = 262144
F1 = 512
CMAX = 12
F2 = 512
GROUPS = 4
TOUT = 131072


def draw_group_of(key, part):
    seeded = jax.random.fold_in(key, 17)
    pick_key, label_key, shuffle_key = jax.random.split(seeded, 3)
    largest = jax.random.randint(pick_key, (), 0, GROUPS)
    offsets = jax.random.randint(label_key, (CHANS,), 0, GROUPS - 1)
    places = jnp.arange(CHANS, dtype=jnp.int32)
    spread_label = (largest + 1 + offsets) % GROUPS
    forced_label = (largest + 1 + places - CMAX) % GROUPS
    labels = jnp.where(places < CMAX, largest, jnp.where(places < CMAX + GROUPS - 1, forced_label, spread_label))
    shuffle = jax.random.permutation(shuffle_key, CHANS)
    return labels[shuffle].astype(jnp.int32)


def place_ends(entries, key, least, top_value):
    extent = entries.shape
    spot = [jax.random.randint(jax.random.fold_in(key, axis), (), 0, extent[axis]) for axis in range(len(extent))]
    entries = entries.at[tuple(spot)].set(least)
    longest = extent.index(max(extent))
    spot[longest] = (spot[longest] + 1) % extent[longest]
    return entries.at[tuple(spot)].set(top_value)


def shard_levels(key, extent, pieces, low, high):
    gain, own = 1.0, jax.random.fold_in(key, 6)
    for position, parts in pieces:
        draws = jnp.exp(jax.random.uniform(jax.random.fold_in(own, position), (parts,), jnp.float32, low / len(pieces), high / len(pieces)))
        gain = gain * jnp.repeat(draws, extent[position] // parts).reshape([-1 if axis == position else 1 for axis in range(len(extent))])
    return gain


def gaussian(rng, dims, scale, limit, pieces=(), kind=jnp.bfloat16):
    level = shard_levels(rng, dims, pieces, -0.22, 0.18) if pieces else 1.0
    drawn = jax.random.normal(rng, dims, jnp.float32) * scale * level
    return jnp.minimum(jnp.maximum(drawn, -limit), limit).astype(kind)


def setup_inputs(seed: int = 0) -> dict:
    splits = jax.random.split(jax.random.key(seed), 5)
    return {
        "voltages": gaussian(splits[0], (BEAMS, CHANS, POLS, 2, NFFT), 1.0, 8.0, ((4, 32),)),
        "chirp_phase": jnp.clip(jax.random.uniform(splits[1], (CHANS, F1, F2), jnp.float32, -3.140625, 3.140625), -3.140625, 3.140625),
        "intersection": place_ends(jax.random.randint(splits[2], (CHANS,), 1, NFFT // 2 + 1), jax.random.fold_in(splits[2], 1), 1, (NFFT // 2 + 1) - 1).astype(jnp.int32),
        "group_of": draw_group_of(jax.random.fold_in(splits[4], 71), 0),
    }


full_turn = 2.0 * math.pi


def channel_power(samples, phase_table, shift_count):
    values = samples.astype(jnp.float32)
    complex_signal = values[:, :, 0, :] + 1j * values[:, :, 1, :]
    spectrum = jnp.fft.fft(complex_signal, axis=-1)
    bins = jnp.arange(NFFT, dtype=jnp.int32)
    low_bin = bins % F1
    high_bin = bins // F1
    ramp = (low_bin * shift_count + F1 * ((high_bin * shift_count) % F2)) % NFFT
    phase_total = jnp.transpose(phase_table).reshape(NFFT) + full_turn * ramp.astype(jnp.float32) / NFFT
    result = jnp.fft.ifft(spectrum * jnp.exp(1j * phase_total), axis=-1)[:, :, :TOUT]
    return jnp.sum(jnp.real(result) ** 2 + jnp.imag(result) ** 2, axis=1)


def reference(voltages, chirp_phase, intersection, group_of):
    powers = lax.map(lambda items: channel_power(items[0], items[1], items[2]),
                     (jnp.moveaxis(voltages, 1, 0), chirp_phase, intersection))
    member = (group_of[None, :] == jnp.arange(GROUPS, dtype=jnp.int32)[:, None]).astype(jnp.float32)
    counts = jnp.sum(member, axis=1)
    totals = jnp.einsum("gc,cbt->bgt", member, powers, precision=lax.Precision.HIGHEST)
    return totals / (2.0 * counts)[None, :, None]
```

```python
import functools
import math

import jax
import jax.numpy as jnp
import numpy as np
from jax import lax
from jax.experimental import pallas as pl
from jax.experimental.pallas import tpu as pltpu
from jax.sharding import PartitionSpec as P

f32 = jnp.float32
bf16 = jnp.bfloat16


def split(values):
    high = values.astype(bf16)
    return high, (values - high.astype(f32)).astype(bf16)


def np_split(values):
    high = values.astype(np.float32).astype(bf16)
    low = (values - high.astype(np.float64)).astype(np.float32).astype(bf16)
    return np.asarray(high), np.asarray(low)


@functools.lru_cache(None)
def tables(f):
    index = np.arange(f)
    product = index[:, None] * index[None, :]
    angle = 2.0 * np.pi * (product % f) / f
    c, s = np.cos(angle), np.sin(angle)
    forward = np.block([[c, -s], [s, c]])
    inverse = np.block([[c, s], [-s, c]])
    twist = 2.0 * np.pi * product / (f * f)
    return (
        *np_split(forward),
        *np_split(inverse),
        np.cos(twist).astype(np.float32),
        np.sin(twist).astype(np.float32),
    )


@functools.lru_cache(None)
def turn_polynomials():
    nodes = 0.125 + 0.13 * np.cos(np.pi * (np.arange(200) + 0.5) / 200)
    root = np.sqrt(np.abs(nodes))
    fits = []
    for values, degree in (
        (np.cos(2 * np.pi * root), 8),
        (np.sin(2 * np.pi * root) / root, 8),
    ):
        keep = nodes > 0
        fit = np.polynomial.Chebyshev.fit(nodes[keep], values[keep], degree, domain=[0, 0.25])
        fits.append([float(x) for x in fit.convert(kind=np.polynomial.Polynomial).coef])
    return fits


def horner(q, coefficients):
    total = jnp.full_like(q, coefficients[-1])
    for x in coefficients[-2::-1]:
        total = total * q + x
    return total


def chirp_tables(shift, phase, k1):
    f = phase.shape[1]
    nfft = f * f
    rows = k1 + lax.broadcasted_iota(jnp.int32, phase.shape, 0)
    cols = lax.broadcasted_iota(jnp.int32, phase.shape, 1)
    ramp = (rows * shift + f * ((cols * shift) & (f - 1))) & (nfft - 1)
    turns = phase * (0.5 / math.pi) + ramp.astype(f32) * (1.0 / nfft)
    rest = turns - jnp.round(turns)
    q = rest * rest
    cos_fit, sin_fit = turn_polynomials()
    scale = 1.0 / nfft
    return horner(q, cos_fit) * scale, horner(q, sin_fit) * (rest * scale)


def mm(a, b):
    return jnp.dot(a, b, preferred_element_type=f32)


def three(values, high, low):
    rows = values.shape[0]
    vh, vl = split(values)
    both = mm(jnp.concatenate([vh, vl], axis=0), high)
    return both[:rows] + both[rows:] + mm(vh, low)


def rows_step(i, z, g2h, g2l, g3h, g3l, tc, ts, cc, cs, vh, vl, tile):
    f = tc.shape[0]
    top = pl.ds(pl.multiple_of(i * tile, tile), tile)
    bot = pl.ds(pl.multiple_of(f + i * tile, tile), tile)
    lhs = jnp.concatenate([g3h[top], g3h[bot], g3l[top], g3l[bot]], axis=0)
    r = mm(lhs, z)
    yr = r[:tile] + r[2 * tile : 3 * tile]
    yi = r[tile : 2 * tile] + r[3 * tile :]
    c, s = tc[top], ts[top]
    spec = three(jnp.concatenate([yr * c + yi * s, yi * c - yr * s], axis=1), g2h[...], g2l[...])
    zr, zi = spec[:, :f], spec[:, f:]
    hc, hs = cc[top], cs[top]
    v = three(jnp.concatenate([zr * hc - zi * hs, zr * hs + zi * hc], axis=1), g3h[...], g3l[...])
    vr, vi = v[:, :f], v[:, f:]
    ah, al = split(vr * c - vi * s)
    vh[top], vl[top] = ah, al
    ah, al = split(vr * s + vi * c)
    vh[bot], vl[bot] = ah, al


def last_step(g2h, g2l, vh, vl):
    f = vh.shape[1]
    half = f // 2
    highs = [g2h[:half], g2h[f : f + half]]
    lhs = jnp.concatenate(highs + [g2l[:half], g2l[f : f + half]], axis=0)
    r = mm(lhs, vh[...])
    sig = r[:f] + r[f:] + mm(jnp.concatenate(highs, axis=0), vl[...])
    sr, si = sig[:half], sig[half:]
    return sr * sr + si * si


def local_kernel(shift, z, phase, g2h, g2l, g3h, g3l, tc, ts, power, cc, cs, vh, vl, *, tile):
    f = phase.shape[0]
    pols = z.shape[0]

    def chirp_step(i, carry):
        rows = pl.ds(pl.multiple_of(i * 64, 64), 64)
        cc[rows], cs[rows] = chirp_tables(shift[0], phase[rows], i * 64)
        return carry

    lax.fori_loop(0, f // 64, chirp_step, 0)
    power[...] = jnp.zeros_like(power)

    def pol_step(p, carry):
        def step(i, inner):
            rows_step(i, z[p], g2h, g2l, g3h, g3l, tc, ts, cc, cs, vh, vl, tile)
            return inner

        lax.fori_loop(0, f // tile, step, 0)
        power[...] += last_step(g2h, g2l, vh, vl)
        return carry

    lax.fori_loop(0, pols, pol_step, 0)


def channel_power(shift, z, phase):
    f = phase.shape[0]
    tile = f // 2
    smem = pl.BlockSpec(memory_space=pltpu.SMEM)
    vmem = pl.BlockSpec(memory_space=pltpu.VMEM)
    return pl.pallas_call(
        functools.partial(local_kernel, tile=tile),
        out_shape=jax.ShapeDtypeStruct((f // 2, f), f32),
        in_specs=[smem] + [vmem] * 8,
        out_specs=vmem,
        scratch_shapes=[
            pltpu.VMEM((f, f), f32),
            pltpu.VMEM((f, f), f32),
            pltpu.VMEM((2 * f, f), bf16),
            pltpu.VMEM((2 * f, f), bf16),
        ],
        compiler_params=pltpu.CompilerParams(vmem_limit_bytes=56 * 1024 * 1024),
    )(shift, z, phase, *(jnp.asarray(t) for t in tables(f)))


def on_device(voltages, chirp_phase, intersection, group_of):
    tm_count = lax.axis_size("tm")
    grp_count = lax.axis_size("grp")
    devices = tm_count * grp_count
    tm_rank = lax.axis_index("tm")
    grp_rank = lax.axis_index("grp")
    me = tm_rank * grp_count + grp_rank
    beams, chans, pols, _, local_len = voltages.shape
    f = chirp_phase.shape[2]
    rows = local_len // f
    groups = 4
    owners = np.arange(chans) * devices // chans
    owned = np.zeros(devices, np.int32)
    owned[owners] = np.arange(chans)
    active = np.zeros(devices, np.float32)
    active[owners] = 1.0
    mine = jnp.asarray(owned)[me]
    out = jnp.take(voltages[0], owned, axis=0)
    got = lax.all_to_all(out, ("tm", "grp"), split_axis=0, concat_axis=0, tiled=True)
    z = jnp.transpose(got.reshape(devices, pols, 2, rows, f), (1, 2, 0, 3, 4)).reshape(pols, 2 * f, f)
    column = jnp.asarray(owned.reshape(tm_count, grp_count))[:, grp_rank]
    phase = lax.all_to_all(
        jnp.take(chirp_phase, column, axis=0), "tm", split_axis=0, concat_axis=0, tiled=True
    ).reshape(f, f)
    power = channel_power(intersection[mine][None], z, phase)
    moved = lax.all_to_all(
        power.reshape(devices, -1), ("tm", "grp"), split_axis=0, concat_axis=0, tiled=True
    )
    member = (group_of[None, :] == jnp.arange(groups, dtype=jnp.int32)[:, None]).astype(f32)
    counts = jnp.sum(member, axis=1, keepdims=True)
    weights = jnp.take(member, owned, axis=1) * active[None, :] / (2.0 * counts)
    result = jnp.sum(weights[:, :, None] * moved[None], axis=1)
    return result[None]


def solution(mesh):
    in_specs = (P(None, None, None, None, ("tm", "grp")), P(None, "tm", None), P(), P())
    out_specs = P(None, None, ("tm", "grp"))
    return jax.shard_map(
        on_device, mesh=mesh, in_specs=in_specs, out_specs=out_specs, check_vma=False
    )
```

```python
import functools
import math

import jax
import jax.numpy as jnp
import numpy as np
from jax import lax
from jax.experimental import pallas as pl
from jax.experimental.pallas import tpu as pltpu
from jax.sharding import PartitionSpec as P

f32 = jnp.float32
bf16 = jnp.bfloat16


def split(values):
    high = values.astype(bf16)
    return high, (values - high.astype(f32)).astype(bf16)


def np_split(values):
    high = values.astype(np.float32).astype(bf16)
    low = (values - high.astype(np.float64)).astype(np.float32).astype(bf16)
    return np.asarray(high), np.asarray(low)


@functools.lru_cache(None)
def tables(f):
    index = np.arange(f)
    product = index[:, None] * index[None, :]
    angle = 2.0 * np.pi * (product % f) / f
    c, s = np.cos(angle), np.sin(angle)
    forward = np.block([[c, -s], [s, c]])
    inverse = np.block([[c, s], [-s, c]])
    twist = 2.0 * np.pi * product / (f * f)
    return (
        *np_split(forward),
        *np_split(inverse),
        np.cos(twist).astype(np.float32),
        np.sin(twist).astype(np.float32),
    )


@functools.lru_cache(None)
def turn_polynomials():
    nodes = 0.125 + 0.13 * np.cos(np.pi * (np.arange(200) + 0.5) / 200)
    root = np.sqrt(np.abs(nodes))
    fits = []
    for values, degree in (
        (np.cos(2 * np.pi * root), 8),
        (np.sin(2 * np.pi * root) / root, 8),
    ):
        keep = nodes > 0
        fit = np.polynomial.Chebyshev.fit(nodes[keep], values[keep], degree, domain=[0, 0.25])
        fits.append([float(x) for x in fit.convert(kind=np.polynomial.Polynomial).coef])
    return fits


def horner(q, coefficients):
    total = jnp.full_like(q, coefficients[-1])
    for x in coefficients[-2::-1]:
        total = total * q + x
    return total


def chirp_tables(shift, phase, k1):
    f = phase.shape[1]
    nfft = f * f
    rows = k1 + lax.broadcasted_iota(jnp.int32, phase.shape, 0)
    cols = lax.broadcasted_iota(jnp.int32, phase.shape, 1)
    ramp = (rows * shift + f * ((cols * shift) & (f - 1))) & (nfft - 1)
    turns = phase * (0.5 / math.pi) + ramp.astype(f32) * (1.0 / nfft)
    rest = turns - jnp.round(turns)
    q = rest * rest
    cos_fit, sin_fit = turn_polynomials()
    scale = 1.0 / nfft
    return horner(q, cos_fit) * scale, horner(q, sin_fit) * (rest * scale)


def mm(a, b):
    return jnp.dot(a, b, preferred_element_type=f32)


def three(values, high, low):
    rows = values.shape[0]
    vh, vl = split(values)
    both = mm(jnp.concatenate([vh, vl], axis=0), high)
    return both[:rows] + both[rows:] + mm(vh, low)


def rows_step(i, z, g2h, g2l, g3h, g3l, tc, ts, cc, cs, vh, vl, tile):
    f = tc.shape[0]
    top = pl.ds(pl.multiple_of(i * tile, tile), tile)
    bot = pl.ds(pl.multiple_of(f + i * tile, tile), tile)
    lhs = jnp.concatenate([g3h[top], g3h[bot], g3l[top], g3l[bot]], axis=0)
    r = mm(lhs, z)
    yr = r[:tile] + r[2 * tile : 3 * tile]
    yi = r[tile : 2 * tile] + r[3 * tile :]
    c, s = tc[top], ts[top]
    spec = three(jnp.concatenate([yr * c + yi * s, yi * c - yr * s], axis=1), g2h[...], g2l[...])
    zr, zi = spec[:, :f], spec[:, f:]
    hc, hs = cc[top], cs[top]
    v = three(jnp.concatenate([zr * hc - zi * hs, zr * hs + zi * hc], axis=1), g3h[...], g3l[...])
    vr, vi = v[:, :f], v[:, f:]
    ah, al = split(vr * c - vi * s)
    vh[top], vl[top] = ah, al
    ah, al = split(vr * s + vi * c)
    vh[bot], vl[bot] = ah, al


def last_step(g2h, g2l, vh, vl):
    f = vh.shape[1]
    half = f // 2
    highs = [g2h[:half], g2h[f : f + half]]
    lhs = jnp.concatenate(highs + [g2l[:half], g2l[f : f + half]], axis=0)
    r = mm(lhs, vh[...])
    sig = r[:f] + r[f:] + mm(jnp.concatenate(highs, axis=0), vl[...])
    sr, si = sig[:half], sig[half:]
    return sr * sr + si * si


def local_kernel(shift, z, phase, g2h, g2l, g3h, g3l, tc, ts, power, cc, cs, vh, vl, *, tile):
    f = phase.shape[0]
    pols = z.shape[0]

    def chirp_step(i, carry):
        rows = pl.ds(pl.multiple_of(i * 64, 64), 64)
        cc[rows], cs[rows] = chirp_tables(shift[0], phase[rows], i * 64)
        return carry

    lax.fori_loop(0, f // 64, chirp_step, 0)
    power[...] = jnp.zeros_like(power)

    def pol_step(p, carry):
        def step(i, inner):
            rows_step(i, z[p], g2h, g2l, g3h, g3l, tc, ts, cc, cs, vh, vl, tile)
            return inner

        lax.fori_loop(0, f // tile, step, 0)
        power[...] += last_step(g2h, g2l, vh, vl)
        return carry

    lax.fori_loop(0, pols, pol_step, 0)


def channel_power(shift, z, phase):
    f = phase.shape[0]
    tile = f // 2
    smem = pl.BlockSpec(memory_space=pltpu.SMEM)
    vmem = pl.BlockSpec(memory_space=pltpu.VMEM)
    return pl.pallas_call(
        functools.partial(local_kernel, tile=tile),
        out_shape=jax.ShapeDtypeStruct((f // 2, f), f32),
        in_specs=[smem] + [vmem] * 8,
        out_specs=vmem,
        scratch_shapes=[
            pltpu.VMEM((f, f), f32),
            pltpu.VMEM((f, f), f32),
            pltpu.VMEM((2 * f, f), bf16),
            pltpu.VMEM((2 * f, f), bf16),
        ],
        compiler_params=pltpu.CompilerParams(vmem_limit_bytes=56 * 1024 * 1024),
    )(shift, z, phase, *(jnp.asarray(t) for t in tables(f)))


MESH = pl.DeviceIdType.MESH


def staggered(chans, tm_count, grp_count):
    return grp_count == 4 and chans == tm_count * (grp_count - 1)


def owner_of(c):
    t, k = lax.div(c, 3), lax.rem(c, 3)
    a = lax.rem(lax.div(t, 2) + lax.rem(t, 2), 2)
    return t, k + a * lax.div(k + 1, 2)


def channel_at(t, j):
    a = lax.rem(lax.div(t, 2) + lax.rem(t, 2), 2)
    return 3 * t + j - a * lax.div(j + 3, 4), j != 3 - 2 * a


def fused_kernel(
    shift, weights, volt, chirp, h_g2h, h_g2l, h_g3h, h_g3l, h_tc, h_ts, out,
    z, phase, gathered, power, g2h, g2l, g3h, g3l, tc, ts, cc, cs, vh, vl,
    table_sem, volt_send, volt_recv, chirp_send, chirp_recv, power_send, power_recv,
    *, tm_count, grp_count, tile,
):
    t, j = lax.axis_index("tm"), lax.axis_index("grp")
    devices = tm_count * grp_count
    me = t * grp_count + j
    chans, pols, _, rows, f = volt.shape
    k_rows = chirp.shape[1]
    t_rows = gathered.shape[1]
    mine, active = channel_at(t, j)

    pairs = [(h_g2h, g2h), (h_g2l, g2l), (h_g3h, g3h), (h_g3l, g3l), (h_tc, tc), (h_ts, ts)]
    loads = [pltpu.make_async_copy(a, b, table_sem.at[i]) for i, (a, b) in enumerate(pairs)]
    for load in loads:
        load.start()

    barrier = pltpu.get_barrier_semaphore()

    def greet(i, carry):
        d = lax.rem(me + i, devices)
        pl.semaphore_signal(
            barrier, inc=1, device_id=(lax.div(d, grp_count), lax.rem(d, grp_count)), device_id_type=MESH
        )
        return carry

    lax.fori_loop(1, devices, greet, 0)
    pl.semaphore_wait(barrier, devices - 1)

    k_slot = pl.ds(pl.multiple_of(t * k_rows, k_rows), k_rows)
    z_slot = pl.ds(pl.multiple_of(me * rows, rows), rows)
    first = 3 * t

    def chirp_copy(c, ot, oj):
        return pltpu.make_async_remote_copy(
            src_ref=chirp.at[c], dst_ref=phase.at[k_slot], send_sem=chirp_send.at[c],
            recv_sem=chirp_recv, device_id=(ot, oj), device_id_type=MESH,
        )

    def volt_copy(c, p, ot, oj):
        return pltpu.make_async_remote_copy(
            src_ref=volt.at[c, p], dst_ref=z.at[p, :, z_slot], send_sem=volt_send.at[p, c],
            recv_sem=volt_recv.at[p], device_id=(ot, oj), device_id_type=MESH,
        )

    def over_channels(start, act):
        def step(i, carry):
            c = lax.rem(start + i, chans)
            ot, oj = owner_of(c)
            act(c, ot, oj)
            return carry

        lax.fori_loop(0, chans, step, 0)

    def send_chirp(c, ot, oj):
        @pl.when((oj == j) & (ot != t))
        def _():
            chirp_copy(c, ot, oj).start()

    over_channels(first, send_chirp)

    @pl.when(active)
    def _():
        pltpu.make_async_copy(chirp.at[mine], phase.at[k_slot], chirp_recv).start()

    def send_pol(p, carry):
        def send_volt(c, ot, oj):
            @pl.when((oj != j) | (ot != t))
            def _():
                volt_copy(c, p, ot, oj).start()

        over_channels(first, send_volt)

        @pl.when(active)
        def _():
            pltpu.make_async_copy(volt.at[mine, p], z.at[p, :, z_slot], volt_recv.at[p]).start()

        return carry

    lax.fori_loop(0, pols, send_pol, 0)
    for load in loads:
        load.wait()

    def power_copy(d):
        return pltpu.make_async_remote_copy(
            src_ref=power.at[pl.ds(pl.multiple_of(d * t_rows, t_rows), t_rows)],
            dst_ref=gathered.at[mine], send_sem=power_send.at[d], recv_sem=power_recv,
            device_id=(lax.div(d, grp_count), lax.rem(d, grp_count)), device_id_type=MESH,
        )

    @pl.when(active)
    def _():
        pltpu.make_async_copy(phase, phase, chirp_recv).wait()

        def chirp_step(i, carry):
            part = pl.ds(pl.multiple_of(i * 64, 64), 64)
            cc[part], cs[part] = chirp_tables(shift[0], phase[part], i * 64)
            return carry

        lax.fori_loop(0, f // 64, chirp_step, 0)
        power[...] = jnp.zeros_like(power)

        def pol_step(p, carry):
            pltpu.make_async_copy(z.at[p], z.at[p], volt_recv.at[p]).wait()

            def step(i, inner):
                samples = z[p].reshape(2 * f, f)
                rows_step(i, samples, g2h, g2l, g3h, g3l, tc, ts, cc, cs, vh, vl, tile)
                return inner

            lax.fori_loop(0, f // tile, step, 0)
            power[...] += last_step(g2h, g2l, vh, vl)
            return carry

        lax.fori_loop(0, pols, pol_step, 0)

        def send_power(i, carry):
            power_copy(lax.rem(me + i, devices)).start()
            return carry

        lax.fori_loop(1, devices, send_power, 0)
        own = power.at[pl.ds(pl.multiple_of(me * t_rows, t_rows), t_rows)]
        pltpu.make_async_copy(own, gathered.at[mine], power_recv).start()

    pltpu.make_async_copy(gathered, gathered, power_recv).wait()
    for g in range(out.shape[0]):
        total = weights[g * chans] * gathered[0]
        for c in range(1, chans):
            total = total + weights[g * chans + c] * gathered[c]
        out[g] = total

    def wait_chirp(c, ot, oj):
        @pl.when((oj == j) & (ot != t))
        def _():
            chirp_copy(c, ot, oj).wait_send()

    def wait_volt(c, ot, oj):
        @pl.when((oj != j) | (ot != t))
        def _():
            for p in range(pols):
                volt_copy(c, p, ot, oj).wait_send()

    over_channels(first, wait_chirp)
    over_channels(first, wait_volt)

    @pl.when(active)
    def _():
        def wait_power(i, carry):
            power_copy(lax.rem(me + i, devices)).wait_send()
            return carry

        lax.fori_loop(1, devices, wait_power, 0)


def fused(shift, weights, volt, chirp, tm_count, grp_count, groups):
    chans, pols, _, rows, f = volt.shape
    devices = tm_count * grp_count
    t_rows = f // 2 // devices
    smem = pl.BlockSpec(memory_space=pltpu.SMEM)
    hbm = pl.BlockSpec(memory_space=pl.ANY)
    dma = pltpu.SemaphoreType.DMA
    square = lambda kind, scale=1: pltpu.VMEM((scale * f, scale * f), kind)
    return pl.pallas_call(
        functools.partial(fused_kernel, tm_count=tm_count, grp_count=grp_count, tile=f // 2),
        out_shape=jax.ShapeDtypeStruct((groups, t_rows, f), f32),
        in_specs=[smem, smem] + [hbm] * 8,
        out_specs=pl.BlockSpec(memory_space=pltpu.VMEM),
        scratch_shapes=[
            pltpu.VMEM((pols, 2, f, f), bf16),
            square(f32),
            pltpu.VMEM((chans, t_rows, f), f32),
            pltpu.VMEM((f // 2, f), f32),
            *[square(bf16, 2)] * 4,
            *[square(f32)] * 4,
            pltpu.VMEM((2 * f, f), bf16),
            pltpu.VMEM((2 * f, f), bf16),
            dma((6,)),
            dma((pols, chans)),
            dma((pols,)),
            dma((chans,)),
            dma,
            dma((devices,)),
            dma,
        ],
        compiler_params=pltpu.CompilerParams(
            vmem_limit_bytes=56 * 1024 * 1024, collective_id=0, has_side_effects=True
        ),
    )(shift, weights, volt, chirp, *(jnp.asarray(t) for t in tables(f)))


def on_device(voltages, chirp_phase, intersection, group_of):
    tm_count = lax.axis_size("tm")
    grp_count = lax.axis_size("grp")
    devices = tm_count * grp_count
    tm_rank = lax.axis_index("tm")
    grp_rank = lax.axis_index("grp")
    me = tm_rank * grp_count + grp_rank
    beams, chans, pols, _, local_len = voltages.shape
    f = chirp_phase.shape[2]
    rows = local_len // f
    groups = 4
    member = (group_of[None, :] == jnp.arange(groups, dtype=jnp.int32)[:, None]).astype(f32)
    shares = member / (2.0 * jnp.sum(member, axis=1, keepdims=True))
    if staggered(chans, tm_count, grp_count) and rows % 16 == 0 and (f // 2) % (8 * devices) == 0:
        mine = channel_at(tm_rank, grp_rank)[0]
        result = fused(
            lax.dynamic_slice(intersection, (mine,), (1,)),
            shares.reshape(-1),
            voltages.reshape(chans, pols, 2, rows, f),
            chirp_phase,
            tm_count,
            grp_count,
            groups,
        )
        return result.reshape(beams, groups, -1)
    owners = np.arange(chans) * devices // chans
    owned = np.zeros(devices, np.int32)
    owned[owners] = np.arange(chans)
    active = np.zeros(devices, np.float32)
    active[owners] = 1.0
    mine = jnp.asarray(owned)[me]
    out = jnp.take(voltages[0], owned, axis=0)
    got = lax.all_to_all(out, ("tm", "grp"), split_axis=0, concat_axis=0, tiled=True)
    z = jnp.transpose(got.reshape(devices, pols, 2, rows, f), (1, 2, 0, 3, 4)).reshape(pols, 2 * f, f)
    column = jnp.asarray(owned.reshape(tm_count, grp_count))[:, grp_rank]
    phase = lax.all_to_all(
        jnp.take(chirp_phase, column, axis=0), "tm", split_axis=0, concat_axis=0, tiled=True
    ).reshape(f, f)
    power = channel_power(intersection[mine][None], z, phase)
    moved = lax.all_to_all(
        power.reshape(devices, -1), ("tm", "grp"), split_axis=0, concat_axis=0, tiled=True
    )
    weights = jnp.take(shares, owned, axis=1) * active[None, :]
    result = jnp.sum(weights[:, :, None] * moved[None], axis=1)
    return result[None]


def solution(mesh):
    in_specs = (P(None, None, None, None, ("tm", "grp")), P(None, "tm", None), P(), P())
    out_specs = P(None, None, ("tm", "grp"))
    return jax.shard_map(
        on_device, mesh=mesh, in_specs=in_specs, out_specs=out_specs, check_vma=False
    )
```

```python
import functools
import math

import jax
import jax.numpy as jnp
import numpy as np
from jax import lax
from jax.experimental import pallas as pl
from jax.experimental.pallas import tpu as pltpu
from jax.sharding import PartitionSpec as P

f32 = jnp.float32
bf16 = jnp.bfloat16


def split(values):
    high = values.astype(bf16)
    return high, (values - high.astype(f32)).astype(bf16)


def np_split(values):
    high = values.astype(np.float32).astype(bf16)
    low = (values - high.astype(np.float64)).astype(np.float32).astype(bf16)
    return np.asarray(high), np.asarray(low)


@functools.lru_cache(None)
def tables(f):
    index = np.arange(f)
    product = index[:, None] * index[None, :]
    angle = 2.0 * np.pi * (product % f) / f
    c, s = np.cos(angle), np.sin(angle)
    forward = np.block([[c, -s], [s, c]])
    inverse = np.block([[c, s], [-s, c]])
    twist = 2.0 * np.pi * product / (f * f)
    return (
        *np_split(forward),
        *np_split(inverse),
        np.cos(twist).astype(np.float32),
        np.sin(twist).astype(np.float32),
    )


@functools.lru_cache(None)
def turn_polynomials():
    nodes = 0.125 + 0.13 * np.cos(np.pi * (np.arange(200) + 0.5) / 200)
    root = np.sqrt(np.abs(nodes))
    fits = []
    for values, degree in (
        (np.cos(2 * np.pi * root), 8),
        (np.sin(2 * np.pi * root) / root, 8),
    ):
        keep = nodes > 0
        fit = np.polynomial.Chebyshev.fit(nodes[keep], values[keep], degree, domain=[0, 0.25])
        fits.append([float(x) for x in fit.convert(kind=np.polynomial.Polynomial).coef])
    return fits


def horner(q, coefficients):
    total = jnp.full_like(q, coefficients[-1])
    for x in coefficients[-2::-1]:
        total = total * q + x
    return total


def chirp_tables(shift, phase, k1):
    f = phase.shape[1]
    nfft = f * f
    rows = k1 + lax.broadcasted_iota(jnp.int32, phase.shape, 0)
    cols = lax.broadcasted_iota(jnp.int32, phase.shape, 1)
    ramp = (rows * shift + f * ((cols * shift) & (f - 1))) & (nfft - 1)
    turns = phase * (0.5 / math.pi) + ramp.astype(f32) * (1.0 / nfft)
    rest = turns - jnp.round(turns)
    q = rest * rest
    cos_fit, sin_fit = turn_polynomials()
    scale = 1.0 / nfft
    return horner(q, cos_fit) * scale, horner(q, sin_fit) * (rest * scale)


def turn_tables(shift, fraction, k1):
    f = fraction.shape[1]
    nfft = f * f
    rows = k1 + lax.broadcasted_iota(jnp.int32, fraction.shape, 0)
    cols = lax.broadcasted_iota(jnp.int32, fraction.shape, 1)
    ramp = rows * shift + f * ((cols * shift) & (f - 1))
    steps = fraction.astype(jnp.int32) * (nfft // 65536) + ramp
    rest = (((steps + nfft // 2) & (nfft - 1)) - nfft // 2).astype(f32) * (1.0 / nfft)
    q = rest * rest
    cos_fit, sin_fit = turn_polynomials()
    scale = 1.0 / nfft
    return horner(q, cos_fit) * scale, horner(q, sin_fit) * (rest * scale)


def mm(a, b):
    return jnp.dot(a, b, preferred_element_type=f32)


def three(values, high, low):
    rows = values.shape[0]
    vh, vl = split(values)
    both = mm(jnp.concatenate([vh, vl], axis=0), high)
    return both[:rows] + both[rows:] + mm(vh, low)


def rows_step(i, z, g2h, g2l, g3h, g3l, tc, ts, cc, cs, vh, vl, tile):
    f = tc.shape[0]
    top = pl.ds(pl.multiple_of(i * tile, tile), tile)
    bot = pl.ds(pl.multiple_of(f + i * tile, tile), tile)
    lhs = jnp.concatenate([g3h[top], g3h[bot], g3l[top], g3l[bot]], axis=0)
    r = mm(lhs, z)
    yr = r[:tile] + r[2 * tile : 3 * tile]
    yi = r[tile : 2 * tile] + r[3 * tile :]
    c, s = tc[top], ts[top]
    spec = three(jnp.concatenate([yr * c + yi * s, yi * c - yr * s], axis=1), g2h[...], g2l[...])
    zr, zi = spec[:, :f], spec[:, f:]
    hc, hs = cc[top], cs[top]
    v = three(jnp.concatenate([zr * hc - zi * hs, zr * hs + zi * hc], axis=1), g3h[...], g3l[...])
    vr, vi = v[:, :f], v[:, f:]
    ah, al = split(vr * c - vi * s)
    vh[top], vl[top] = ah, al
    ah, al = split(vr * s + vi * c)
    vh[bot], vl[bot] = ah, al


def last_step(g2h, g2l, vh, vl):
    f = vh.shape[1]
    half = f // 2
    highs = [g2h[:half], g2h[f : f + half]]
    lhs = jnp.concatenate(highs + [g2l[:half], g2l[f : f + half]], axis=0)
    r = mm(lhs, vh[...])
    sig = r[:f] + r[f:] + mm(jnp.concatenate(highs, axis=0), vl[...])
    sr, si = sig[:half], sig[half:]
    return sr * sr + si * si


def local_kernel(shift, z, phase, g2h, g2l, g3h, g3l, tc, ts, power, cc, cs, vh, vl, *, tile):
    f = phase.shape[0]
    pols = z.shape[0]

    def chirp_step(i, carry):
        rows = pl.ds(pl.multiple_of(i * 64, 64), 64)
        cc[rows], cs[rows] = chirp_tables(shift[0], phase[rows], i * 64)
        return carry

    lax.fori_loop(0, f // 64, chirp_step, 0)
    power[...] = jnp.zeros_like(power)

    def pol_step(p, carry):
        def step(i, inner):
            rows_step(i, z[p], g2h, g2l, g3h, g3l, tc, ts, cc, cs, vh, vl, tile)
            return inner

        lax.fori_loop(0, f // tile, step, 0)
        power[...] += last_step(g2h, g2l, vh, vl)
        return carry

    lax.fori_loop(0, pols, pol_step, 0)


def channel_power(shift, z, phase):
    f = phase.shape[0]
    tile = f // 2
    smem = pl.BlockSpec(memory_space=pltpu.SMEM)
    vmem = pl.BlockSpec(memory_space=pltpu.VMEM)
    return pl.pallas_call(
        functools.partial(local_kernel, tile=tile),
        out_shape=jax.ShapeDtypeStruct((f // 2, f), f32),
        in_specs=[smem] + [vmem] * 8,
        out_specs=vmem,
        scratch_shapes=[
            pltpu.VMEM((f, f), f32),
            pltpu.VMEM((f, f), f32),
            pltpu.VMEM((2 * f, f), bf16),
            pltpu.VMEM((2 * f, f), bf16),
        ],
        compiler_params=pltpu.CompilerParams(vmem_limit_bytes=56 * 1024 * 1024),
    )(shift, z, phase, *(jnp.asarray(t) for t in tables(f)))


MESH = pl.DeviceIdType.MESH


def staggered(chans, tm_count, grp_count):
    return grp_count == 4 and chans == tm_count * (grp_count - 1)


def owner_of(c):
    t, k = lax.div(c, 3), lax.rem(c, 3)
    a = lax.rem(lax.div(t, 2) + lax.rem(t, 2), 2)
    return t, k + a * lax.div(k + 1, 2)


def channel_at(t, j):
    a = lax.rem(lax.div(t, 2) + lax.rem(t, 2), 2)
    return 3 * t + j - a * lax.div(j + 3, 4), j != 3 - 2 * a


def fused_kernel(
    shifts, group_of, volt, chirp, h_g2h, h_g2l, h_g3h, h_g3l, h_tc, h_ts, out,
    rows32, rows16, z, phase, gathered, power, g2h, g2l, g3h, g3l, tc, ts, cc, cs, vh, vl,
    table_sem, rows_sem, volt_send, volt_recv, chirp_send, chirp_recv, power_send, power_recv,
    *, tm_count, grp_count, tile,
):
    t, j = lax.axis_index("tm"), lax.axis_index("grp")
    devices = tm_count * grp_count
    me = t * grp_count + j
    chans, pols, _, rows, f = volt.shape
    k_rows = chirp.shape[1]
    t_rows = gathered.shape[1]
    mine, active = channel_at(t, j)

    pairs = [(h_g2h, g2h), (h_g2l, g2l), (h_g3h, g3h), (h_g3l, g3l), (h_tc, tc), (h_ts, ts)]
    loads = [pltpu.make_async_copy(a, b, table_sem.at[i]) for i, (a, b) in enumerate(pairs)]
    for load in loads:
        load.start()

    def over_column(act):
        def step(i, carry):
            c, owned = channel_at(i, j)

            @pl.when(owned)
            def _():
                act(i, c)

            return carry

        lax.fori_loop(0, tm_count, step, 0)

    def load_rows(i, c):
        return pltpu.make_async_copy(chirp.at[c], rows32.at[i], rows_sem.at[i])

    over_column(lambda i, c: load_rows(i, c).start())
    barrier = pltpu.get_barrier_semaphore()

    def greet(i, carry):
        d = lax.rem(me + i, devices)
        pl.semaphore_signal(
            barrier, inc=1, device_id=(lax.div(d, grp_count), lax.rem(d, grp_count)), device_id_type=MESH
        )
        return carry

    lax.fori_loop(1, devices, greet, 0)
    pl.semaphore_wait(barrier, devices - 1)

    k_slot = pl.ds(pl.multiple_of(t * k_rows, k_rows), k_rows)
    z_slot = pl.ds(pl.multiple_of(me * rows, rows), rows)
    first = 3 * t

    def chirp_copy(i):
        return pltpu.make_async_remote_copy(
            src_ref=rows16.at[i], dst_ref=phase.at[k_slot], send_sem=chirp_send.at[i],
            recv_sem=chirp_recv, device_id=(i, j), device_id_type=MESH,
        )

    def volt_copy(c, p, ot, oj):
        return pltpu.make_async_remote_copy(
            src_ref=volt.at[c, p], dst_ref=z.at[p, :, z_slot], send_sem=volt_send.at[p, c],
            recv_sem=volt_recv.at[p], device_id=(ot, oj), device_id_type=MESH,
        )

    def over_channels(start, act):
        def step(i, carry):
            c = lax.rem(start + i, chans)
            ot, oj = owner_of(c)
            act(c, ot, oj)
            return carry

        lax.fori_loop(0, chans, step, 0)

    def elsewhere(ot, oj):
        return (oj != j) | (ot != t)

    def send_first(c, ot, oj):
        @pl.when(elsewhere(ot, oj))
        def _():
            volt_copy(c, 0, ot, oj).start()

    over_channels(first, send_first)

    @pl.when(active)
    def _():
        def own(p, carry):
            pltpu.make_async_copy(volt.at[mine, p], z.at[p, :, z_slot], volt_recv.at[p]).start()
            return carry

        lax.fori_loop(0, pols, own, 0)

    def send_rows(i, c):
        load_rows(i, c).wait()
        rows16[i] = jnp.round(rows32[i] * (32768.0 / math.pi)).astype(jnp.int32).astype(jnp.int16)

        @pl.when(i != t)
        def _():
            chirp_copy(i).start()

        @pl.when(i == t)
        def _():
            pltpu.make_async_copy(rows16.at[i], phase.at[k_slot], chirp_recv).start()

    over_column(send_rows)

    for p in range(1, pols):
        def send_next(c, ot, oj):
            @pl.when(elsewhere(ot, oj))
            def _():
                volt_copy(c, p - 1, ot, oj).wait_send()
                volt_copy(c, p, ot, oj).start()

        over_channels(first, send_next)

    for load in loads:
        load.wait()

    def power_copy(d):
        return pltpu.make_async_remote_copy(
            src_ref=power.at[pl.ds(pl.multiple_of(d * t_rows, t_rows), t_rows)],
            dst_ref=gathered.at[mine], send_sem=power_send.at[d], recv_sem=power_recv,
            device_id=(lax.div(d, grp_count), lax.rem(d, grp_count)), device_id_type=MESH,
        )

    @pl.when(active)
    def _():
        pltpu.make_async_copy(phase, phase, chirp_recv).wait()

        def chirp_step(i, carry):
            part = pl.ds(pl.multiple_of(i * 64, 64), 64)
            cc[part], cs[part] = turn_tables(shifts[mine], phase[part], i * 64)
            return carry

        lax.fori_loop(0, f // 64, chirp_step, 0)
        power[...] = jnp.zeros_like(power)

        def pol_step(p, carry):
            pltpu.make_async_copy(z.at[p], z.at[p], volt_recv.at[p]).wait()

            def step(i, inner):
                samples = z[p].reshape(2 * f, f)
                rows_step(i, samples, g2h, g2l, g3h, g3l, tc, ts, cc, cs, vh, vl, tile)
                return inner

            lax.fori_loop(0, f // tile, step, 0)
            power[...] += last_step(g2h, g2l, vh, vl)
            return carry

        lax.fori_loop(0, pols, pol_step, 0)

        def send_power(i, carry):
            power_copy(lax.rem(me + i, devices)).start()
            return carry

        lax.fori_loop(1, devices, send_power, 0)
        own = power.at[pl.ds(pl.multiple_of(me * t_rows, t_rows), t_rows)]
        pltpu.make_async_copy(own, gathered.at[mine], power_recv).start()

    pltpu.make_async_copy(gathered, gathered, power_recv).wait()
    for g in range(out.shape[0]):
        total = jnp.zeros((t_rows, f), f32)
        count = jnp.int32(0)
        for c in range(chans):
            member = (group_of[c] == g).astype(jnp.int32)
            count = count + member
            total = total + member.astype(f32) * gathered[c]
        total = total / jnp.full((t_rows, f), 2 * count, jnp.int32).astype(f32)
        for r in range(t_rows):
            out[g : g + 1, r * f : (r + 1) * f] = total[r : r + 1]

    def wait_rows(i, c):
        @pl.when(i != t)
        def _():
            chirp_copy(i).wait_send()

    def wait_volt(c, ot, oj):
        @pl.when(elsewhere(ot, oj))
        def _():
            volt_copy(c, pols - 1, ot, oj).wait_send()

    over_column(wait_rows)
    over_channels(first, wait_volt)

    @pl.when(active)
    def _():
        def wait_power(i, carry):
            power_copy(lax.rem(me + i, devices)).wait_send()
            return carry

        lax.fori_loop(1, devices, wait_power, 0)


def fused(shifts, group_of, volt, chirp, tm_count, grp_count, groups):
    chans, pols, _, rows, f = volt.shape
    devices = tm_count * grp_count
    t_rows = f // 2 // devices
    smem = pl.BlockSpec(memory_space=pltpu.SMEM)
    hbm = pl.BlockSpec(memory_space=pl.ANY)
    dma = pltpu.SemaphoreType.DMA
    square = lambda kind, scale=1: pltpu.VMEM((scale * f, scale * f), kind)
    return pl.pallas_call(
        functools.partial(fused_kernel, tm_count=tm_count, grp_count=grp_count, tile=f // 2),
        out_shape=jax.ShapeDtypeStruct((groups, t_rows * f), f32),
        in_specs=[smem, smem] + [hbm] * 8,
        out_specs=pl.BlockSpec(memory_space=pltpu.VMEM),
        scratch_shapes=[
            pltpu.VMEM((tm_count, chirp.shape[1], f), f32),
            pltpu.VMEM((tm_count, chirp.shape[1], f), jnp.int16),
            pltpu.VMEM((pols, 2, f, f), bf16),
            square(jnp.int16),
            pltpu.VMEM((chans, t_rows, f), f32),
            pltpu.VMEM((f // 2, f), f32),
            *[square(bf16, 2)] * 4,
            *[square(f32)] * 4,
            pltpu.VMEM((2 * f, f), bf16),
            pltpu.VMEM((2 * f, f), bf16),
            dma((6,)),
            dma((tm_count,)),
            dma((pols, chans)),
            dma((pols,)),
            dma((tm_count,)),
            dma,
            dma((devices,)),
            dma,
        ],
        compiler_params=pltpu.CompilerParams(
            vmem_limit_bytes=56 * 1024 * 1024, collective_id=0, has_side_effects=True
        ),
    )(shifts, group_of, volt, chirp, *(jnp.asarray(t) for t in tables(f)))


def on_device(voltages, chirp_phase, intersection, group_of):
    tm_count = lax.axis_size("tm")
    grp_count = lax.axis_size("grp")
    devices = tm_count * grp_count
    tm_rank = lax.axis_index("tm")
    grp_rank = lax.axis_index("grp")
    me = tm_rank * grp_count + grp_rank
    beams, chans, pols, _, local_len = voltages.shape
    f = chirp_phase.shape[2]
    rows = local_len // f
    groups = 4
    member = (group_of[None, :] == jnp.arange(groups, dtype=jnp.int32)[:, None]).astype(f32)
    shares = member / (2.0 * jnp.sum(member, axis=1, keepdims=True))
    whole_tiles = rows % 16 == 0 and chirp_phase.shape[1] % 16 == 0 and (f // 2) % (8 * devices) == 0
    if staggered(chans, tm_count, grp_count) and whole_tiles and f * f % 65536 == 0:
        result = fused(
            intersection,
            group_of,
            voltages.reshape(chans, pols, 2, rows, f),
            chirp_phase,
            tm_count,
            grp_count,
            groups,
        )
        return result.reshape(beams, groups, -1)
    owners = np.arange(chans) * devices // chans
    owned = np.zeros(devices, np.int32)
    owned[owners] = np.arange(chans)
    active = np.zeros(devices, np.float32)
    active[owners] = 1.0
    mine = jnp.asarray(owned)[me]
    out = jnp.take(voltages[0], owned, axis=0)
    got = lax.all_to_all(out, ("tm", "grp"), split_axis=0, concat_axis=0, tiled=True)
    z = jnp.transpose(got.reshape(devices, pols, 2, rows, f), (1, 2, 0, 3, 4)).reshape(pols, 2 * f, f)
    column = jnp.asarray(owned.reshape(tm_count, grp_count))[:, grp_rank]
    phase = lax.all_to_all(
        jnp.take(chirp_phase, column, axis=0), "tm", split_axis=0, concat_axis=0, tiled=True
    ).reshape(f, f)
    power = channel_power(intersection[mine][None], z, phase)
    moved = lax.all_to_all(
        power.reshape(devices, -1), ("tm", "grp"), split_axis=0, concat_axis=0, tiled=True
    )
    weights = jnp.take(shares, owned, axis=1) * active[None, :]
    result = jnp.sum(weights[:, :, None] * moved[None], axis=1)
    return result[None]


def solution(mesh):
    in_specs = (P(None, None, None, None, ("tm", "grp")), P(None, "tm", None), P(), P())
    out_specs = P(None, None, ("tm", "grp"))
    return jax.shard_map(
        on_device, mesh=mesh, in_specs=in_specs, out_specs=out_specs, check_vma=False
    )
```

```python
import functools
import math

import jax
import jax.numpy as jnp
import numpy as np
from jax import lax
from jax.experimental import pallas as pl
from jax.experimental.pallas import tpu as pltpu
from jax.sharding import PartitionSpec as P

f32 = jnp.float32
bf16 = jnp.bfloat16


def split(values):
    high = values.astype(bf16)
    return high, (values - high.astype(f32)).astype(bf16)


def np_split(values):
    high = values.astype(np.float32).astype(bf16)
    low = (values - high.astype(np.float64)).astype(np.float32).astype(bf16)
    return np.asarray(high), np.asarray(low)


def halves(c, s, sign):
    return np.block([[c, sign * s], [-sign * s, c]])


@functools.lru_cache(None)
def tables(f):
    h = f // 2
    index = np.arange(f)
    product = index[:, None] * index[None, :]
    angle = 2.0 * np.pi * (product % f) / f
    c, s = np.cos(angle), np.sin(angle)
    left = np.stack(np_split(np.block([[c, s], [-s, c]])))
    ahead, back, last = [], [], []
    for odd in (0, 1):
        ahead.append(np.stack(np_split(halves(c[:h, odd::2], s[:h, odd::2], -1))))
        back.append(np.stack(np_split(halves(c[odd::2, :h], s[odd::2, :h], 1))))
        part = slice(odd, h, 2)
        last.append(np.stack(np_split(np.block([[c[part, :h], -s[part, :h]], [s[part, :h], c[part, :h]]]))))
    twist = 2.0 * np.pi * product / (f * f)
    turned = np.stack([np.cos(twist), np.sin(twist)]).astype(np.float32)
    order = np.eye(f)[:, np.concatenate([index[::2], index[1::2]])].astype(bf16)
    return left, np.stack(ahead), np.stack(back), np.stack(last), turned, np.asarray(order)


def column_ids(shape):
    h = shape[1] // 2
    cols = lax.broadcasted_iota(jnp.int32, shape, 1)
    return 2 * (cols & (h - 1)) + (cols >= h).astype(jnp.int32)


@functools.lru_cache(None)
def turn_polynomials():
    nodes = 0.125 + 0.13 * np.cos(np.pi * (np.arange(200) + 0.5) / 200)
    root = np.sqrt(np.abs(nodes))
    fits = []
    for values, degree in (
        (np.cos(2 * np.pi * root), 8),
        (np.sin(2 * np.pi * root) / root, 8),
    ):
        keep = nodes > 0
        fit = np.polynomial.Chebyshev.fit(nodes[keep], values[keep], degree, domain=[0, 0.25])
        fits.append([float(x) for x in fit.convert(kind=np.polynomial.Polynomial).coef])
    return fits


def horner(q, coefficients):
    total = jnp.full_like(q, coefficients[-1])
    for x in coefficients[-2::-1]:
        total = total * q + x
    return total


def chirp_tables(shift, phase, k1):
    f = phase.shape[1]
    nfft = f * f
    rows = k1 + lax.broadcasted_iota(jnp.int32, phase.shape, 0)
    cols = column_ids(phase.shape)
    ramp = (rows * shift + f * ((cols * shift) & (f - 1))) & (nfft - 1)
    turns = phase * (0.5 / math.pi) + ramp.astype(f32) * (1.0 / nfft)
    rest = turns - jnp.round(turns)
    q = rest * rest
    cos_fit, sin_fit = turn_polynomials()
    scale = 1.0 / nfft
    return horner(q, cos_fit) * scale, horner(q, sin_fit) * (rest * scale)


def turn_tables(shift, fraction, order, k1):
    whole = fraction.astype(jnp.int32)
    upper = whole >> 8
    parts = jnp.concatenate([upper, whole - upper * 256], axis=0).astype(f32).astype(bf16)
    moved = mm(parts, order).astype(jnp.int32)
    fraction = moved[: whole.shape[0]] * 256 + moved[whole.shape[0] :]
    f = fraction.shape[1]
    nfft = f * f
    rows = k1 + lax.broadcasted_iota(jnp.int32, fraction.shape, 0)
    cols = column_ids(fraction.shape)
    ramp = rows * shift + f * ((cols * shift) & (f - 1))
    steps = fraction * (nfft // 65536) + ramp
    rest = (((steps + nfft // 2) & (nfft - 1)) - nfft // 2).astype(f32) * (1.0 / nfft)
    q = rest * rest
    cos_fit, sin_fit = turn_polynomials()
    scale = 1.0 / nfft
    return horner(q, cos_fit) * scale, horner(q, sin_fit) * (rest * scale)


def mm(a, b):
    return jnp.dot(a, b, preferred_element_type=f32)


def three(values, high, low):
    rows = values.shape[0]
    vh, vl = split(values)
    both = mm(jnp.concatenate([vh, vl], axis=0), high)
    return both[:rows] + both[rows:] + mm(vh, low)


def rows_step(i, z, left, ahead, back, turned, cc, cs, v, tile):
    f = cc.shape[0]
    h = f // 2
    top = pl.ds(pl.multiple_of(i * tile, tile), tile)
    bot = pl.ds(pl.multiple_of(f + i * tile, tile), tile)
    lhs = jnp.concatenate([left[0, top], left[0, bot], left[1, top], left[1, bot]], axis=0)
    r = mm(lhs, z)
    yr = r[:tile] + r[2 * tile : 3 * tile]
    yi = r[tile : 2 * tile] + r[3 * tile :]
    c, s = turned[0, top], turned[1, top]
    ar, ai = yr * c + yi * s, yi * c - yr * s
    found = []
    for odd in (0, 1):
        sign = 1 - 2 * odd
        pair = [ar[:, :h] + sign * ar[:, h:], ai[:, :h] + sign * ai[:, h:]]
        spec = three(jnp.concatenate(pair, axis=1), ahead[odd, 0], ahead[odd, 1])
        zr, zi = spec[:, :h], spec[:, h:]
        cols = slice(odd * h, (odd + 1) * h)
        hc, hs = cc[top, cols], cs[top, cols]
        pair = [zr * hc - zi * hs, zr * hs + zi * hc]
        found.append(three(jnp.concatenate(pair, axis=1), back[odd, 0], back[odd, 1]))
    plus, minus = found[0] + found[1], found[0] - found[1]
    vr = jnp.concatenate([plus[:, :h], minus[:, :h]], axis=1)
    vi = jnp.concatenate([plus[:, h:], minus[:, h:]], axis=1)
    v[top] = vr * c - vi * s
    v[bot] = vr * s + vi * c


def last_step(last, v, power):
    f = v.shape[1]
    h, q = f // 2, f // 4
    for odd in (0, 1):
        sign = 1 - 2 * odd
        both = [v[:h] + sign * v[h:f], v[f : f + h] + sign * v[f + h :]]
        vh, vl = split(jnp.concatenate(both, axis=0))
        high, low = last[odd, 0], last[odd, 1]
        r = mm(jnp.concatenate([high, low], axis=0), vh)
        sig = r[:h] + r[h:] + mm(high, vl)
        sr, si = sig[:q], sig[q:]
        power[odd] += sr * sr + si * si


def local_kernel(shift, z, phase, left, ahead, back, last, turned, order, power, cc, cs, v, *, tile):
    f = phase.shape[0]
    pols = z.shape[0]

    def chirp_step(i, carry):
        rows = pl.ds(pl.multiple_of(i * 64, 64), 64)
        cc[rows], cs[rows] = chirp_tables(shift[0], phase[rows], i * 64)
        return carry

    lax.fori_loop(0, f // 64, chirp_step, 0)
    power[...] = jnp.zeros_like(power)

    def pol_step(p, carry):
        def step(i, inner):
            rows_step(i, z[p], left, ahead, back, turned, cc, cs, v, tile)
            return inner

        lax.fori_loop(0, f // tile, step, 0)
        last_step(last, v, power)
        return carry

    lax.fori_loop(0, pols, pol_step, 0)


def channel_power(shift, z, phase):
    f = phase.shape[0]
    tile = f // 2
    smem = pl.BlockSpec(memory_space=pltpu.SMEM)
    vmem = pl.BlockSpec(memory_space=pltpu.VMEM)
    phase = jnp.concatenate([phase[:, ::2], phase[:, 1::2]], axis=1)
    power = pl.pallas_call(
        functools.partial(local_kernel, tile=tile),
        out_shape=jax.ShapeDtypeStruct((2, f // 4, f), f32),
        in_specs=[smem] + [vmem] * 8,
        out_specs=vmem,
        scratch_shapes=[
            pltpu.VMEM((f, f), f32),
            pltpu.VMEM((f, f), f32),
            pltpu.VMEM((2 * f, f), f32),
        ],
        compiler_params=pltpu.CompilerParams(vmem_limit_bytes=56 * 1024 * 1024),
    )(shift, z, phase, *(jnp.asarray(t) for t in tables(f)))
    return jnp.swapaxes(power, 0, 1).reshape(f // 2, f)


MESH = pl.DeviceIdType.MESH


def staggered(chans, tm_count, grp_count):
    return grp_count == 4 and chans == tm_count * (grp_count - 1)


def owner_of(c):
    t, k = lax.div(c, 3), lax.rem(c, 3)
    a = lax.rem(lax.div(t, 2) + lax.rem(t, 2), 2)
    return t, k + a * lax.div(k + 1, 2)


def channel_at(t, j):
    a = lax.rem(lax.div(t, 2) + lax.rem(t, 2), 2)
    return 3 * t + j - a * lax.div(j + 3, 4), j != 3 - 2 * a


def fused_kernel(
    shifts, group_of, volt, chirp, h_left, h_ahead, h_back, h_last, h_turned, h_order, out,
    rows32, rows16, z, phase, gathered, summed, power, left, ahead, back, last, turned, order, cc, cs, v,
    table_sem, rows_sem, volt_send, volt_recv, chirp_send, chirp_recv, power_send, power_recv,
    *, tm_count, grp_count, tile,
):
    t, j = lax.axis_index("tm"), lax.axis_index("grp")
    devices = tm_count * grp_count
    me = t * grp_count + j
    chans, pols, _, rows, f = volt.shape
    k_rows = chirp.shape[1]
    t_rows = gathered.shape[1]
    mine, active = channel_at(t, j)

    pairs = [(h_left, left), (h_ahead, ahead), (h_back, back)]
    pairs += [(h_last, last), (h_turned, turned), (h_order, order)]
    loads = [pltpu.make_async_copy(a, b, table_sem.at[i]) for i, (a, b) in enumerate(pairs)]
    for load in loads:
        load.start()

    def over_column(act):
        def step(i, carry):
            c, owned = channel_at(i, j)

            @pl.when(owned)
            def _():
                act(i, c)

            return carry

        lax.fori_loop(0, tm_count, step, 0)

    def load_rows(i, c):
        return pltpu.make_async_copy(chirp.at[c], rows32.at[i], rows_sem.at[i])

    over_column(lambda i, c: load_rows(i, c).start())
    barrier = pltpu.get_barrier_semaphore()

    def greet(i, carry):
        d = lax.rem(me + i, devices)
        pl.semaphore_signal(
            barrier, inc=1, device_id=(lax.div(d, grp_count), lax.rem(d, grp_count)), device_id_type=MESH
        )
        return carry

    lax.fori_loop(1, devices, greet, 0)
    pl.semaphore_wait(barrier, devices - 1)

    k_slot = pl.ds(pl.multiple_of(t * k_rows, k_rows), k_rows)
    z_slot = pl.ds(pl.multiple_of(me * rows, rows), rows)
    first = 3 * t

    def chirp_copy(i):
        return pltpu.make_async_remote_copy(
            src_ref=rows16.at[i], dst_ref=phase.at[k_slot], send_sem=chirp_send.at[i],
            recv_sem=chirp_recv, device_id=(i, j), device_id_type=MESH,
        )

    def volt_copy(c, p, ot, oj):
        return pltpu.make_async_remote_copy(
            src_ref=volt.at[c, p], dst_ref=z.at[p, :, z_slot], send_sem=volt_send.at[p, c],
            recv_sem=volt_recv.at[p], device_id=(ot, oj), device_id_type=MESH,
        )

    def over_channels(start, act):
        def step(i, carry):
            c = lax.rem(start + i, chans)
            ot, oj = owner_of(c)
            act(c, ot, oj)
            return carry

        lax.fori_loop(0, chans, step, 0)

    def elsewhere(ot, oj):
        return (oj != j) | (ot != t)

    def send_first(c, ot, oj):
        @pl.when(elsewhere(ot, oj))
        def _():
            volt_copy(c, 0, ot, oj).start()

    over_channels(first, send_first)

    @pl.when(active)
    def _():
        def own(p, carry):
            pltpu.make_async_copy(volt.at[mine, p], z.at[p, :, z_slot], volt_recv.at[p]).start()
            return carry

        lax.fori_loop(0, pols, own, 0)

    def send_rows(i, c):
        load_rows(i, c).wait()
        rows16[i] = jnp.round(rows32[i] * (32768.0 / math.pi)).astype(jnp.int32).astype(jnp.int16)

        @pl.when(i != t)
        def _():
            chirp_copy(i).start()

        @pl.when(i == t)
        def _():
            pltpu.make_async_copy(rows16.at[i], phase.at[k_slot], chirp_recv).start()

    over_column(send_rows)

    for p in range(1, pols):
        def send_next(c, ot, oj):
            @pl.when(elsewhere(ot, oj))
            def _():
                volt_copy(c, p - 1, ot, oj).wait_send()
                volt_copy(c, p, ot, oj).start()

        over_channels(first, send_next)

    for load in loads:
        load.wait()

    def power_copy(d):
        return pltpu.make_async_remote_copy(
            src_ref=power.at[d],
            dst_ref=gathered.at[mine], send_sem=power_send.at[d], recv_sem=power_recv,
            device_id=(lax.div(d, grp_count), lax.rem(d, grp_count)), device_id_type=MESH,
        )

    @pl.when(active)
    def _():
        pltpu.make_async_copy(phase, phase, chirp_recv).wait()

        def chirp_step(i, carry):
            part = pl.ds(pl.multiple_of(i * 64, 64), 64)
            cc[part], cs[part] = turn_tables(shifts[mine], phase[part], order[...], i * 64)
            return carry

        lax.fori_loop(0, f // 64, chirp_step, 0)
        summed[...] = jnp.zeros_like(summed)

        def pol_step(p, carry):
            pltpu.make_async_copy(z.at[p], z.at[p], volt_recv.at[p]).wait()

            def step(i, inner):
                samples = z[p].reshape(2 * f, f)
                rows_step(i, samples, left, ahead, back, turned, cc, cs, v, tile)
                return inner

            lax.fori_loop(0, f // tile, step, 0)
            last_step(last, v, summed)
            return carry

        lax.fori_loop(0, pols, pol_step, 0)

        q = t_rows // 2
        for d in range(devices):
            for odd in (0, 1):
                power[d, odd * q : (odd + 1) * q] = summed[odd, d * q : (d + 1) * q]

        def send_power(i, carry):
            power_copy(lax.rem(me + i, devices)).start()
            return carry

        lax.fori_loop(1, devices, send_power, 0)
        pltpu.make_async_copy(power.at[me], gathered.at[mine], power_recv).start()

    pltpu.make_async_copy(gathered, gathered, power_recv).wait()
    for g in range(out.shape[0]):
        total = jnp.zeros((t_rows, f), f32)
        count = jnp.int32(0)
        for c in range(chans):
            member = (group_of[c] == g).astype(jnp.int32)
            count = count + member
            total = total + member.astype(f32) * gathered[c]
        total = total / jnp.full((t_rows, f), 2 * count, jnp.int32).astype(f32)
        for r in range(t_rows):
            when = 2 * r if r < t_rows // 2 else 2 * r - t_rows + 1
            out[g : g + 1, when * f : (when + 1) * f] = total[r : r + 1]

    def wait_rows(i, c):
        @pl.when(i != t)
        def _():
            chirp_copy(i).wait_send()

    def wait_volt(c, ot, oj):
        @pl.when(elsewhere(ot, oj))
        def _():
            volt_copy(c, pols - 1, ot, oj).wait_send()

    over_column(wait_rows)
    over_channels(first, wait_volt)

    @pl.when(active)
    def _():
        def wait_power(i, carry):
            power_copy(lax.rem(me + i, devices)).wait_send()
            return carry

        lax.fori_loop(1, devices, wait_power, 0)


def fused(shifts, group_of, volt, chirp, tm_count, grp_count, groups):
    chans, pols, _, rows, f = volt.shape
    devices = tm_count * grp_count
    t_rows = f // 2 // devices
    smem = pl.BlockSpec(memory_space=pltpu.SMEM)
    hbm = pl.BlockSpec(memory_space=pl.ANY)
    dma = pltpu.SemaphoreType.DMA
    square = lambda kind: pltpu.VMEM((f, f), kind)
    return pl.pallas_call(
        functools.partial(fused_kernel, tm_count=tm_count, grp_count=grp_count, tile=f // 2),
        out_shape=jax.ShapeDtypeStruct((groups, t_rows * f), f32),
        in_specs=[smem, smem] + [hbm] * 8,
        out_specs=pl.BlockSpec(memory_space=pltpu.VMEM),
        scratch_shapes=[
            pltpu.VMEM((tm_count, chirp.shape[1], f), f32),
            pltpu.VMEM((tm_count, chirp.shape[1], f), jnp.int16),
            pltpu.VMEM((pols, 2, f, f), bf16),
            square(jnp.int16),
            pltpu.VMEM((chans, t_rows, f), f32),
            pltpu.VMEM((2, f // 4, f), f32),
            pltpu.VMEM((devices, t_rows, f), f32),
            *[pltpu.VMEM(t.shape, t.dtype) for t in tables(f)],
            square(f32),
            square(f32),
            pltpu.VMEM((2 * f, f), f32),
            dma((6,)),
            dma((tm_count,)),
            dma((pols, chans)),
            dma((pols,)),
            dma((tm_count,)),
            dma,
            dma((devices,)),
            dma,
        ],
        compiler_params=pltpu.CompilerParams(
            vmem_limit_bytes=56 * 1024 * 1024, collective_id=0, has_side_effects=True
        ),
    )(shifts, group_of, volt, chirp, *(jnp.asarray(t) for t in tables(f)))


def on_device(voltages, chirp_phase, intersection, group_of):
    tm_count = lax.axis_size("tm")
    grp_count = lax.axis_size("grp")
    devices = tm_count * grp_count
    tm_rank = lax.axis_index("tm")
    grp_rank = lax.axis_index("grp")
    me = tm_rank * grp_count + grp_rank
    beams, chans, pols, _, local_len = voltages.shape
    f = chirp_phase.shape[2]
    rows = local_len // f
    groups = 4
    member = (group_of[None, :] == jnp.arange(groups, dtype=jnp.int32)[:, None]).astype(f32)
    shares = member / (2.0 * jnp.sum(member, axis=1, keepdims=True))
    whole_tiles = rows % 16 == 0 and chirp_phase.shape[1] % 16 == 0 and (f // 2) % (8 * devices) == 0
    if staggered(chans, tm_count, grp_count) and whole_tiles and f * f % 65536 == 0:
        result = fused(
            intersection,
            group_of,
            voltages.reshape(chans, pols, 2, rows, f),
            chirp_phase,
            tm_count,
            grp_count,
            groups,
        )
        return result.reshape(beams, groups, -1)
    owners = np.arange(chans) * devices // chans
    owned = np.zeros(devices, np.int32)
    owned[owners] = np.arange(chans)
    active = np.zeros(devices, np.float32)
    active[owners] = 1.0
    mine = jnp.asarray(owned)[me]
    out = jnp.take(voltages[0], owned, axis=0)
    got = lax.all_to_all(out, ("tm", "grp"), split_axis=0, concat_axis=0, tiled=True)
    z = jnp.transpose(got.reshape(devices, pols, 2, rows, f), (1, 2, 0, 3, 4)).reshape(pols, 2 * f, f)
    column = jnp.asarray(owned.reshape(tm_count, grp_count))[:, grp_rank]
    phase = lax.all_to_all(
        jnp.take(chirp_phase, column, axis=0), "tm", split_axis=0, concat_axis=0, tiled=True
    ).reshape(f, f)
    power = channel_power(intersection[mine][None], z, phase)
    moved = lax.all_to_all(
        power.reshape(devices, -1), ("tm", "grp"), split_axis=0, concat_axis=0, tiled=True
    )
    weights = jnp.take(shares, owned, axis=1) * active[None, :]
    result = jnp.sum(weights[:, :, None] * moved[None], axis=1)
    return result[None]


def solution(mesh):
    in_specs = (P(None, None, None, None, ("tm", "grp")), P(None, "tm", None), P(), P())
    out_specs = P(None, None, ("tm", "grp"))
    return jax.shard_map(
        on_device, mesh=mesh, in_specs=in_specs, out_specs=out_specs, check_vma=False
    )
```

```python
import functools
import math

import jax
import jax.numpy as jnp
import numpy as np
from jax import lax
from jax.experimental import pallas as pl
from jax.experimental.pallas import tpu as pltpu
from jax.sharding import PartitionSpec as P

f32 = jnp.float32
bf16 = jnp.bfloat16


def split(values):
    high = values.astype(bf16)
    return high, (values - high.astype(f32)).astype(bf16)


def np_split(values):
    high = values.astype(np.float32).astype(bf16)
    low = (values - high.astype(np.float64)).astype(np.float32).astype(bf16)
    return np.asarray(high), np.asarray(low)


def halves(c, s, sign):
    return np.block([[c, sign * s], [-sign * s, c]])


@functools.lru_cache(None)
def tables(f):
    h = f // 2
    index = np.arange(f)
    product = index[:, None] * index[None, :]
    angle = 2.0 * np.pi * (product % f) / f
    c, s = np.cos(angle), np.sin(angle)
    left = np.stack(np_split(np.block([[c, s], [-s, c]])))
    ahead, back, last = [], [], []
    for odd in (0, 1):
        ahead.append(np.stack(np_split(halves(c[:h, odd::2], s[:h, odd::2], -1))))
        back.append(np.stack(np_split(halves(c[odd::2, :h], s[odd::2, :h], 1))))
        part = slice(odd, h, 2)
        last.append(np.stack(np_split(np.block([[c[part, :h], -s[part, :h]], [s[part, :h], c[part, :h]]]))))
    twist = 2.0 * np.pi * product / (f * f)
    turned = np.stack([np.cos(twist), np.sin(twist)]).astype(np.float32)
    order = np.eye(f)[:, np.concatenate([index[::2], index[1::2]])].astype(bf16)
    return left, np.stack(ahead), np.stack(back), np.stack(last), turned, np.asarray(order)


def column_ids(shape):
    h = shape[1] // 2
    cols = lax.broadcasted_iota(jnp.int32, shape, 1)
    return 2 * (cols & (h - 1)) + (cols >= h).astype(jnp.int32)


@functools.lru_cache(None)
def turn_polynomials():
    nodes = 0.125 + 0.13 * np.cos(np.pi * (np.arange(200) + 0.5) / 200)
    root = np.sqrt(np.abs(nodes))
    fits = []
    for values, degree in (
        (np.cos(2 * np.pi * root), 8),
        (np.sin(2 * np.pi * root) / root, 8),
    ):
        keep = nodes > 0
        fit = np.polynomial.Chebyshev.fit(nodes[keep], values[keep], degree, domain=[0, 0.25])
        fits.append([float(x) for x in fit.convert(kind=np.polynomial.Polynomial).coef])
    return fits


def horner(q, coefficients):
    total = jnp.full_like(q, coefficients[-1])
    for x in coefficients[-2::-1]:
        total = total * q + x
    return total


def chirp_tables(shift, phase, k1):
    f = phase.shape[1]
    nfft = f * f
    rows = k1 + lax.broadcasted_iota(jnp.int32, phase.shape, 0)
    cols = column_ids(phase.shape)
    ramp = (rows * shift + f * ((cols * shift) & (f - 1))) & (nfft - 1)
    turns = phase * (0.5 / math.pi) + ramp.astype(f32) * (1.0 / nfft)
    rest = turns - jnp.round(turns)
    q = rest * rest
    cos_fit, sin_fit = turn_polynomials()
    scale = 1.0 / nfft
    return horner(q, cos_fit) * scale, horner(q, sin_fit) * (rest * scale)


def turn_tables(shift, fraction, order, k1):
    whole = fraction.astype(jnp.int32)
    upper = whole >> 8
    parts = jnp.concatenate([upper, whole - upper * 256], axis=0).astype(f32).astype(bf16)
    moved = mm(parts, order).astype(jnp.int32)
    fraction = moved[: whole.shape[0]] * 256 + moved[whole.shape[0] :]
    f = fraction.shape[1]
    nfft = f * f
    rows = k1 + lax.broadcasted_iota(jnp.int32, fraction.shape, 0)
    cols = column_ids(fraction.shape)
    ramp = rows * shift + f * ((cols * shift) & (f - 1))
    steps = fraction * (nfft // 65536) + ramp
    rest = (((steps + nfft // 2) & (nfft - 1)) - nfft // 2).astype(f32) * (1.0 / nfft)
    q = rest * rest
    cos_fit, sin_fit = turn_polynomials()
    scale = 1.0 / nfft
    return horner(q, cos_fit) * scale, horner(q, sin_fit) * (rest * scale)


def mm(a, b):
    return jnp.dot(a, b, preferred_element_type=f32)


def three(values, high, low):
    rows = values.shape[0]
    vh, vl = split(values)
    both = mm(jnp.concatenate([vh, vl], axis=0), high)
    return both[:rows] + both[rows:] + mm(vh, low)


def rows_step(i, z, left, ahead, back, turned, cc, cs, v, tile):
    f = cc.shape[0]
    h = f // 2
    top = pl.ds(pl.multiple_of(i * tile, tile), tile)
    bot = pl.ds(pl.multiple_of(f + i * tile, tile), tile)
    lhs = jnp.concatenate([left[0, top], left[0, bot], left[1, top], left[1, bot]], axis=0)
    r = mm(lhs, z)
    yr = r[:tile] + r[2 * tile : 3 * tile]
    yi = r[tile : 2 * tile] + r[3 * tile :]
    c, s = turned[0, top], turned[1, top]
    ar, ai = yr * c + yi * s, yi * c - yr * s
    found = []
    for odd in (0, 1):
        sign = 1 - 2 * odd
        pair = [ar[:, :h] + sign * ar[:, h:], ai[:, :h] + sign * ai[:, h:]]
        spec = three(jnp.concatenate(pair, axis=1), ahead[odd, 0], ahead[odd, 1])
        zr, zi = spec[:, :h], spec[:, h:]
        cols = slice(odd * h, (odd + 1) * h)
        hc, hs = cc[top, cols], cs[top, cols]
        pair = [zr * hc - zi * hs, zr * hs + zi * hc]
        found.append(three(jnp.concatenate(pair, axis=1), back[odd, 0], back[odd, 1]))
    plus, minus = found[0] + found[1], found[0] - found[1]
    vr = jnp.concatenate([plus[:, :h], minus[:, :h]], axis=1)
    vi = jnp.concatenate([plus[:, h:], minus[:, h:]], axis=1)
    v[top] = vr * c - vi * s
    v[bot] = vr * s + vi * c


def last_step(last, v, power):
    f = v.shape[1]
    h, q = f // 2, f // 4
    for odd in (0, 1):
        sign = 1 - 2 * odd
        both = [v[:h] + sign * v[h:f], v[f : f + h] + sign * v[f + h :]]
        vh, vl = split(jnp.concatenate(both, axis=0))
        high, low = last[odd, 0], last[odd, 1]
        r = mm(jnp.concatenate([high, low], axis=0), vh)
        sig = r[:h] + r[h:] + mm(high, vl)
        sr, si = sig[:q], sig[q:]
        power[odd] += sr * sr + si * si


def local_kernel(shift, z, phase, left, ahead, back, last, turned, order, power, cc, cs, v, *, tile):
    f = phase.shape[0]
    pols = z.shape[0]

    def chirp_step(i, carry):
        rows = pl.ds(pl.multiple_of(i * 64, 64), 64)
        cc[rows], cs[rows] = chirp_tables(shift[0], phase[rows], i * 64)
        return carry

    lax.fori_loop(0, f // 64, chirp_step, 0)
    power[...] = jnp.zeros_like(power)

    def pol_step(p, carry):
        def step(i, inner):
            rows_step(i, z[p], left, ahead, back, turned, cc, cs, v, tile)
            return inner

        lax.fori_loop(0, f // tile, step, 0)
        last_step(last, v, power)
        return carry

    lax.fori_loop(0, pols, pol_step, 0)


def channel_power(shift, z, phase):
    f = phase.shape[0]
    tile = f // 2
    smem = pl.BlockSpec(memory_space=pltpu.SMEM)
    vmem = pl.BlockSpec(memory_space=pltpu.VMEM)
    phase = jnp.concatenate([phase[:, ::2], phase[:, 1::2]], axis=1)
    power = pl.pallas_call(
        functools.partial(local_kernel, tile=tile),
        out_shape=jax.ShapeDtypeStruct((2, f // 4, f), f32),
        in_specs=[smem] + [vmem] * 8,
        out_specs=vmem,
        scratch_shapes=[
            pltpu.VMEM((f, f), f32),
            pltpu.VMEM((f, f), f32),
            pltpu.VMEM((2 * f, f), f32),
        ],
        compiler_params=pltpu.CompilerParams(vmem_limit_bytes=56 * 1024 * 1024),
    )(shift, z, phase, *(jnp.asarray(t) for t in tables(f)))
    return jnp.swapaxes(power, 0, 1).reshape(f // 2, f)


MESH = pl.DeviceIdType.MESH


def staggered(chans, tm_count, grp_count):
    return grp_count == 4 and chans == tm_count * (grp_count - 1)


def owner_of(c):
    t, k = lax.div(c, 3), lax.rem(c, 3)
    a = lax.rem(lax.div(t, 2) + lax.rem(t, 2), 2)
    return t, k + a * lax.div(k + 1, 2)


def channel_at(t, j):
    a = lax.rem(lax.div(t, 2) + lax.rem(t, 2), 2)
    return 3 * t + j - a * lax.div(j + 3, 4), j != 3 - 2 * a


def fused_kernel(
    shifts, group_of, volt, chirp, h_left, h_ahead, h_back, h_last, h_turned, h_order, out,
    raw, staged, rows32, rows16, z, phase, gathered, summed, power, left, ahead, back, last, turned, order, cc, cs, v,
    raw_sem, table_sem, rows_sem, volt_send, volt_recv, chirp_send, chirp_recv, power_send, power_recv,
    *, tm_count, grp_count, tile,
):
    t, j = lax.axis_index("tm"), lax.axis_index("grp")
    devices = tm_count * grp_count
    me = t * grp_count + j
    chans, pols, _, rows, f = staged.shape
    k_rows = chirp.shape[1]
    t_rows = gathered.shape[1]
    mine, active = channel_at(t, j)

    first = 3 * t
    fetch = pltpu.make_async_copy(volt, raw, raw_sem)
    fetch.start()
    pairs = [(h_left, left), (h_ahead, ahead), (h_back, back)]
    pairs += [(h_last, last), (h_turned, turned), (h_order, order)]
    loads = [pltpu.make_async_copy(a, b, table_sem.at[i]) for i, (a, b) in enumerate(pairs)]
    for load in loads:
        load.start()

    def over_column(act):
        def step(i, carry):
            c, owned = channel_at(i, j)

            @pl.when(owned)
            def _():
                act(i, c)

            return carry

        lax.fori_loop(0, tm_count, step, 0)

    def load_rows(i, c):
        return pltpu.make_async_copy(chirp.at[c], rows32.at[i], rows_sem.at[i])

    over_column(lambda i, c: load_rows(i, c).start())
    barrier = pltpu.get_barrier_semaphore()

    def greet(i, carry):
        d = lax.rem(me + i, devices)
        pl.semaphore_signal(
            barrier, inc=1, device_id=(lax.div(d, grp_count), lax.rem(d, grp_count)), device_id_type=MESH
        )
        return carry

    lax.fori_loop(1, devices, greet, 0)

    def stage(i, p):
        c = lax.rem(first + i, chans)
        staged[c, p] = raw[c, p].astype(f32).reshape(2, rows, f).astype(bf16)

    def stage_early(i, carry):
        stage(i, 0)
        return carry

    early = chans // 3
    fetch.wait()
    lax.fori_loop(0, early, stage_early, 0)
    pl.semaphore_wait(barrier, devices - 1)

    k_slot = pl.ds(pl.multiple_of(t * k_rows, k_rows), k_rows)
    z_slot = pl.ds(pl.multiple_of(me * rows, rows), rows)

    def chirp_copy(i):
        return pltpu.make_async_remote_copy(
            src_ref=rows16.at[i], dst_ref=phase.at[k_slot], send_sem=chirp_send.at[i],
            recv_sem=chirp_recv, device_id=(i, j), device_id_type=MESH,
        )

    def volt_copy(c, p, ot, oj):
        return pltpu.make_async_remote_copy(
            src_ref=staged.at[c, p], dst_ref=z.at[p, :, z_slot], send_sem=volt_send.at[p, c],
            recv_sem=volt_recv.at[p], device_id=(ot, oj), device_id_type=MESH,
        )

    def over_channels(start, act):
        def step(i, carry):
            c = lax.rem(start + i, chans)
            ot, oj = owner_of(c)
            act(i, c, ot, oj)
            return carry

        lax.fori_loop(0, chans, step, 0)

    def elsewhere(ot, oj):
        return (oj != j) | (ot != t)

    def send_first(i, c, ot, oj):
        @pl.when(elsewhere(ot, oj))
        def _():
            volt_copy(c, 0, ot, oj).start()

        @pl.when(i + early < chans)
        def _():
            stage(i + early, 0)

    over_channels(first, send_first)

    def own(p):
        @pl.when(active)
        def _():
            pltpu.make_async_copy(staged.at[mine, p], z.at[p, :, z_slot], volt_recv.at[p]).start()

    own(0)

    def send_rows(i, c):
        load_rows(i, c).wait()
        rows16[i] = jnp.round(rows32[i] * (32768.0 / math.pi)).astype(jnp.int32).astype(jnp.int16)

        @pl.when(i != t)
        def _():
            chirp_copy(i).start()

        @pl.when(i == t)
        def _():
            pltpu.make_async_copy(rows16.at[i], phase.at[k_slot], chirp_recv).start()

    over_column(send_rows)

    for p in range(1, pols):
        def stage_next(i, carry):
            stage(i, p)
            return carry

        lax.fori_loop(0, chans, stage_next, 0)
        own(p)

        def send_next(i, c, ot, oj):
            @pl.when(elsewhere(ot, oj))
            def _():
                volt_copy(c, p - 1, ot, oj).wait_send()
                volt_copy(c, p, ot, oj).start()

        over_channels(first, send_next)

    for load in loads:
        load.wait()

    def power_copy(d):
        return pltpu.make_async_remote_copy(
            src_ref=power.at[d],
            dst_ref=gathered.at[mine], send_sem=power_send.at[d], recv_sem=power_recv,
            device_id=(lax.div(d, grp_count), lax.rem(d, grp_count)), device_id_type=MESH,
        )

    @pl.when(active)
    def _():
        pltpu.make_async_copy(phase, phase, chirp_recv).wait()

        def chirp_step(i, carry):
            part = pl.ds(pl.multiple_of(i * 64, 64), 64)
            cc[part], cs[part] = turn_tables(shifts[mine], phase[part], order[...], i * 64)
            return carry

        lax.fori_loop(0, f // 64, chirp_step, 0)
        summed[...] = jnp.zeros_like(summed)

        def pol_step(p, carry):
            pltpu.make_async_copy(z.at[p], z.at[p], volt_recv.at[p]).wait()

            def step(i, inner):
                samples = z[p].reshape(2 * f, f)
                rows_step(i, samples, left, ahead, back, turned, cc, cs, v, tile)
                return inner

            lax.fori_loop(0, f // tile, step, 0)
            last_step(last, v, summed)
            return carry

        lax.fori_loop(0, pols, pol_step, 0)

        q = t_rows // 2
        for d in range(devices):
            for odd in (0, 1):
                power[d, odd * q : (odd + 1) * q] = summed[odd, d * q : (d + 1) * q]

        def send_power(i, carry):
            power_copy(lax.rem(me + i, devices)).start()
            return carry

        lax.fori_loop(1, devices, send_power, 0)
        pltpu.make_async_copy(power.at[me], gathered.at[mine], power_recv).start()

    pltpu.make_async_copy(gathered, gathered, power_recv).wait()
    for g in range(out.shape[0]):
        total = jnp.zeros((t_rows, f), f32)
        count = jnp.int32(0)
        for c in range(chans):
            member = (group_of[c] == g).astype(jnp.int32)
            count = count + member
            total = total + member.astype(f32) * gathered[c]
        total = total / jnp.full((t_rows, f), 2 * count, jnp.int32).astype(f32)
        for r in range(t_rows):
            when = 2 * r if r < t_rows // 2 else 2 * r - t_rows + 1
            out[g : g + 1, when * f : (when + 1) * f] = total[r : r + 1]

    def wait_rows(i, c):
        @pl.when(i != t)
        def _():
            chirp_copy(i).wait_send()

    def wait_volt(i, c, ot, oj):
        @pl.when(elsewhere(ot, oj))
        def _():
            volt_copy(c, pols - 1, ot, oj).wait_send()

    over_column(wait_rows)
    over_channels(first, wait_volt)

    @pl.when(active)
    def _():
        def wait_power(i, carry):
            power_copy(lax.rem(me + i, devices)).wait_send()
            return carry

        lax.fori_loop(1, devices, wait_power, 0)


def fused(shifts, group_of, volt, chirp, tm_count, grp_count, groups):
    chans, pols, _, local_len = volt.shape
    f = chirp.shape[2]
    rows = local_len // f
    devices = tm_count * grp_count
    t_rows = f // 2 // devices
    smem = pl.BlockSpec(memory_space=pltpu.SMEM)
    hbm = pl.BlockSpec(memory_space=pl.ANY)
    dma = pltpu.SemaphoreType.DMA
    square = lambda kind: pltpu.VMEM((f, f), kind)
    return pl.pallas_call(
        functools.partial(fused_kernel, tm_count=tm_count, grp_count=grp_count, tile=f // 2),
        out_shape=jax.ShapeDtypeStruct((groups, t_rows * f), f32),
        in_specs=[smem, smem] + [hbm] * 8,
        out_specs=pl.BlockSpec(memory_space=pltpu.VMEM),
        scratch_shapes=[
            pltpu.VMEM(volt.shape, bf16),
            pltpu.VMEM((chans, pols, 2, rows, f), bf16),
            pltpu.VMEM((tm_count, chirp.shape[1], f), f32),
            pltpu.VMEM((tm_count, chirp.shape[1], f), jnp.int16),
            pltpu.VMEM((pols, 2, f, f), bf16),
            square(jnp.int16),
            pltpu.VMEM((chans, t_rows, f), f32),
            pltpu.VMEM((2, f // 4, f), f32),
            pltpu.VMEM((devices, t_rows, f), f32),
            *[pltpu.VMEM(t.shape, t.dtype) for t in tables(f)],
            square(f32),
            square(f32),
            pltpu.VMEM((2 * f, f), f32),
            dma,
            dma((6,)),
            dma((tm_count,)),
            dma((pols, chans)),
            dma((pols,)),
            dma((tm_count,)),
            dma,
            dma((devices,)),
            dma,
        ],
        compiler_params=pltpu.CompilerParams(
            vmem_limit_bytes=56 * 1024 * 1024, collective_id=0, has_side_effects=True
        ),
    )(shifts, group_of, volt, chirp, *(jnp.asarray(t) for t in tables(f)))


def on_device(voltages, chirp_phase, intersection, group_of):
    tm_count = lax.axis_size("tm")
    grp_count = lax.axis_size("grp")
    devices = tm_count * grp_count
    tm_rank = lax.axis_index("tm")
    grp_rank = lax.axis_index("grp")
    me = tm_rank * grp_count + grp_rank
    beams, chans, pols, _, local_len = voltages.shape
    f = chirp_phase.shape[2]
    rows = local_len // f
    groups = 4
    member = (group_of[None, :] == jnp.arange(groups, dtype=jnp.int32)[:, None]).astype(f32)
    shares = member / (2.0 * jnp.sum(member, axis=1, keepdims=True))
    whole_tiles = rows % 16 == 0 and chirp_phase.shape[1] % 16 == 0 and (f // 2) % (8 * devices) == 0
    if staggered(chans, tm_count, grp_count) and whole_tiles and f * f % 65536 == 0:
        result = fused(
            intersection,
            group_of,
            voltages[0],
            chirp_phase,
            tm_count,
            grp_count,
            groups,
        )
        return result.reshape(beams, groups, -1)
    owners = np.arange(chans) * devices // chans
    owned = np.zeros(devices, np.int32)
    owned[owners] = np.arange(chans)
    active = np.zeros(devices, np.float32)
    active[owners] = 1.0
    mine = jnp.asarray(owned)[me]
    out = jnp.take(voltages[0], owned, axis=0)
    got = lax.all_to_all(out, ("tm", "grp"), split_axis=0, concat_axis=0, tiled=True)
    z = jnp.transpose(got.reshape(devices, pols, 2, rows, f), (1, 2, 0, 3, 4)).reshape(pols, 2 * f, f)
    column = jnp.asarray(owned.reshape(tm_count, grp_count))[:, grp_rank]
    phase = lax.all_to_all(
        jnp.take(chirp_phase, column, axis=0), "tm", split_axis=0, concat_axis=0, tiled=True
    ).reshape(f, f)
    power = channel_power(intersection[mine][None], z, phase)
    moved = lax.all_to_all(
        power.reshape(devices, -1), ("tm", "grp"), split_axis=0, concat_axis=0, tiled=True
    )
    weights = jnp.take(shares, owned, axis=1) * active[None, :]
    result = jnp.sum(weights[:, :, None] * moved[None], axis=1)
    return result[None]


def solution(mesh):
    in_specs = (P(None, None, None, None, ("tm", "grp")), P(None, "tm", None), P(), P())
    out_specs = P(None, None, ("tm", "grp"))
    return jax.shard_map(
        on_device, mesh=mesh, in_specs=in_specs, out_specs=out_specs, check_vma=False
    )
```

```python
import functools
import math

import jax
import jax.numpy as jnp
import numpy as np
from jax import lax
from jax.experimental import pallas as pl
from jax.experimental.pallas import tpu as pltpu
from jax.sharding import PartitionSpec as P

f32 = jnp.float32
bf16 = jnp.bfloat16


def split(values):
    high = values.astype(bf16)
    return high, (values - high.astype(f32)).astype(bf16)


def np_split(values):
    high = values.astype(np.float32).astype(bf16)
    low = (values - high.astype(np.float64)).astype(np.float32).astype(bf16)
    return np.asarray(high), np.asarray(low)


def halves(c, s, sign):
    return np.block([[c, sign * s], [-sign * s, c]])


@functools.lru_cache(None)
def tables(f):
    h = f // 2
    index = np.arange(f)
    product = index[:, None] * index[None, :]
    angle = 2.0 * np.pi * (product % f) / f
    c, s = np.cos(angle), np.sin(angle)
    left = np.stack(np_split(np.block([[c, s], [-s, c]])))
    ahead, back, last = [], [], []
    for odd in (0, 1):
        ahead.append(np.stack(np_split(halves(c[:h, odd::2], s[:h, odd::2], -1))))
        back.append(np.stack(np_split(halves(c[odd::2, :h], s[odd::2, :h], 1))))
        part = slice(odd, h, 2)
        last.append(np.stack(np_split(np.block([[c[part, :h], -s[part, :h]], [s[part, :h], c[part, :h]]]))))
    twist = 2.0 * np.pi * product / (f * f)
    turned = np.stack([np.cos(twist), np.sin(twist)]).astype(np.float32)
    order = np.eye(f)[:, np.concatenate([index[::2], index[1::2]])].astype(bf16)
    return left, np.stack(ahead), np.stack(back), np.stack(last), turned, np.asarray(order)


def column_ids(shape):
    h = shape[1] // 2
    cols = lax.broadcasted_iota(jnp.int32, shape, 1)
    return 2 * (cols & (h - 1)) + (cols >= h).astype(jnp.int32)


@functools.lru_cache(None)
def turn_polynomials():
    nodes = 0.125 + 0.13 * np.cos(np.pi * (np.arange(200) + 0.5) / 200)
    root = np.sqrt(np.abs(nodes))
    fits = []
    for values, degree in (
        (np.cos(2 * np.pi * root), 8),
        (np.sin(2 * np.pi * root) / root, 8),
    ):
        keep = nodes > 0
        fit = np.polynomial.Chebyshev.fit(nodes[keep], values[keep], degree, domain=[0, 0.25])
        fits.append([float(x) for x in fit.convert(kind=np.polynomial.Polynomial).coef])
    return fits


def horner(q, coefficients):
    total = jnp.full_like(q, coefficients[-1])
    for x in coefficients[-2::-1]:
        total = total * q + x
    return total


def chirp_tables(shift, phase, k1):
    f = phase.shape[1]
    nfft = f * f
    rows = k1 + lax.broadcasted_iota(jnp.int32, phase.shape, 0)
    cols = column_ids(phase.shape)
    ramp = (rows * shift + f * ((cols * shift) & (f - 1))) & (nfft - 1)
    turns = phase * (0.5 / math.pi) + ramp.astype(f32) * (1.0 / nfft)
    rest = turns - jnp.round(turns)
    q = rest * rest
    cos_fit, sin_fit = turn_polynomials()
    scale = 1.0 / nfft
    return horner(q, cos_fit) * scale, horner(q, sin_fit) * (rest * scale)


def turn_tables(shift, fraction, order, k1):
    whole = fraction.astype(jnp.int32)
    upper = whole >> 8
    parts = jnp.concatenate([upper, whole - upper * 256], axis=0).astype(f32).astype(bf16)
    moved = mm(parts, order).astype(jnp.int32)
    fraction = moved[: whole.shape[0]] * 256 + moved[whole.shape[0] :]
    f = fraction.shape[1]
    nfft = f * f
    rows = k1 + lax.broadcasted_iota(jnp.int32, fraction.shape, 0)
    cols = column_ids(fraction.shape)
    ramp = rows * shift + f * ((cols * shift) & (f - 1))
    steps = fraction * (nfft // 65536) + ramp
    rest = (((steps + nfft // 2) & (nfft - 1)) - nfft // 2).astype(f32) * (1.0 / nfft)
    q = rest * rest
    cos_fit, sin_fit = turn_polynomials()
    scale = 1.0 / nfft
    return horner(q, cos_fit) * scale, horner(q, sin_fit) * (rest * scale)


def mm(a, b):
    return jnp.dot(a, b, preferred_element_type=f32)


def three(values, high, low):
    rows = values.shape[0]
    vh, vl = split(values)
    both = mm(jnp.concatenate([vh, vl], axis=0), high)
    return both[:rows] + both[rows:] + mm(vh, low)


def rows_step(i, z, left, ahead, back, turned, cc, cs, v, tile):
    f = cc.shape[0]
    h = f // 2
    top = pl.ds(pl.multiple_of(i * tile, tile), tile)
    bot = pl.ds(pl.multiple_of(f + i * tile, tile), tile)
    lhs = jnp.concatenate([left[0, top], left[0, bot], left[1, top], left[1, bot]], axis=0)
    r = mm(lhs, z)
    yr = r[:tile] + r[2 * tile : 3 * tile]
    yi = r[tile : 2 * tile] + r[3 * tile :]
    c, s = turned[0, top], turned[1, top]
    ar, ai = yr * c + yi * s, yi * c - yr * s
    found = []
    for odd in (0, 1):
        sign = 1 - 2 * odd
        pair = [ar[:, :h] + sign * ar[:, h:], ai[:, :h] + sign * ai[:, h:]]
        spec = three(jnp.concatenate(pair, axis=1), ahead[odd, 0], ahead[odd, 1])
        zr, zi = spec[:, :h], spec[:, h:]
        cols = slice(odd * h, (odd + 1) * h)
        hc, hs = cc[top, cols], cs[top, cols]
        pair = [zr * hc - zi * hs, zr * hs + zi * hc]
        found.append(three(jnp.concatenate(pair, axis=1), back[odd, 0], back[odd, 1]))
    plus, minus = found[0] + found[1], found[0] - found[1]
    vr = jnp.concatenate([plus[:, :h], minus[:, :h]], axis=1)
    vi = jnp.concatenate([plus[:, h:], minus[:, h:]], axis=1)
    v[top] = vr * c - vi * s
    v[bot] = vr * s + vi * c


def last_step(last, v, power):
    f = v.shape[1]
    h, q = f // 2, f // 4
    for odd in (0, 1):
        sign = 1 - 2 * odd
        both = [v[:h] + sign * v[h:f], v[f : f + h] + sign * v[f + h :]]
        vh, vl = split(jnp.concatenate(both, axis=0))
        high, low = last[odd, 0], last[odd, 1]
        r = mm(jnp.concatenate([high, low], axis=0), vh)
        sig = r[:h] + r[h:] + mm(high, vl)
        sr, si = sig[:q], sig[q:]
        power[odd] += sr * sr + si * si


def local_kernel(shift, z, phase, left, ahead, back, last, turned, order, power, cc, cs, v, *, tile):
    f = phase.shape[0]
    pols = z.shape[0]

    def chirp_step(i, carry):
        rows = pl.ds(pl.multiple_of(i * 64, 64), 64)
        cc[rows], cs[rows] = chirp_tables(shift[0], phase[rows], i * 64)
        return carry

    lax.fori_loop(0, f // 64, chirp_step, 0)
    power[...] = jnp.zeros_like(power)

    def pol_step(p, carry):
        def step(i, inner):
            rows_step(i, z[p], left, ahead, back, turned, cc, cs, v, tile)
            return inner

        lax.fori_loop(0, f // tile, step, 0)
        last_step(last, v, power)
        return carry

    lax.fori_loop(0, pols, pol_step, 0)


def channel_power(shift, z, phase):
    f = phase.shape[0]
    tile = f // 2
    smem = pl.BlockSpec(memory_space=pltpu.SMEM)
    vmem = pl.BlockSpec(memory_space=pltpu.VMEM)
    phase = jnp.concatenate([phase[:, ::2], phase[:, 1::2]], axis=1)
    power = pl.pallas_call(
        functools.partial(local_kernel, tile=tile),
        out_shape=jax.ShapeDtypeStruct((2, f // 4, f), f32),
        in_specs=[smem] + [vmem] * 8,
        out_specs=vmem,
        scratch_shapes=[
            pltpu.VMEM((f, f), f32),
            pltpu.VMEM((f, f), f32),
            pltpu.VMEM((2 * f, f), f32),
        ],
        compiler_params=pltpu.CompilerParams(vmem_limit_bytes=56 * 1024 * 1024),
    )(shift, z, phase, *(jnp.asarray(t) for t in tables(f)))
    return jnp.swapaxes(power, 0, 1).reshape(f // 2, f)


MESH = pl.DeviceIdType.MESH


def staggered(chans, tm_count, grp_count):
    return grp_count == 4 and chans == tm_count * (grp_count - 1) and tm_count % 2 == 0


def owner_of(c):
    t, k = lax.div(c, 3), lax.rem(c, 3)
    a = lax.rem(lax.div(t, 2) + lax.rem(t, 2), 2)
    return t, k + a * lax.div(k + 1, 2)


def far_first(i, count, t, tm_count, shift=0):
    per, half = count // 2, tm_count // 2
    side = lax.rem(lax.div(t, half) + 1 + lax.div(i, per), 2)
    return side * per + lax.rem(i + lax.rem(t, half) * (count // tm_count) + shift, per)


def channel_at(t, j):
    a = lax.rem(lax.div(t, 2) + lax.rem(t, 2), 2)
    return 3 * t + j - a * lax.div(j + 3, 4), j != 3 - 2 * a


def fused_kernel(
    shifts, group_of, volt, chirp, h_left, h_ahead, h_back, h_last, h_turned, h_order, out,
    raw, staged, rows32, rows16, z, phase, gathered, summed, power, left, ahead, back, last, turned, order, cc, cs, v,
    raw_sem, table_sem, rows_sem, volt_send, volt_recv, chirp_send, chirp_recv, power_send, power_recv,
    *, tm_count, grp_count, tile,
):
    t, j = lax.axis_index("tm"), lax.axis_index("grp")
    devices = tm_count * grp_count
    me = t * grp_count + j
    chans, pols, _, rows, f = staged.shape
    k_rows = chirp.shape[1]
    t_rows = gathered.shape[1]
    mine, active = channel_at(t, j)

    fetch = pltpu.make_async_copy(volt, raw, raw_sem)
    fetch.start()
    pairs = [(h_left, left), (h_ahead, ahead), (h_back, back)]
    pairs += [(h_last, last), (h_turned, turned), (h_order, order)]
    loads = [pltpu.make_async_copy(a, b, table_sem.at[i]) for i, (a, b) in enumerate(pairs)]
    for load in loads:
        load.start()

    def over_column(act):
        def step(turn, carry):
            i = far_first(turn, tm_count, t, tm_count)
            c, owned = channel_at(i, j)

            @pl.when(owned)
            def _():
                act(i, c)

            return carry

        lax.fori_loop(0, tm_count, step, 0)

    def load_rows(i, c):
        return pltpu.make_async_copy(chirp.at[c], rows32.at[i], rows_sem.at[i])

    over_column(lambda i, c: load_rows(i, c).start())
    barrier = pltpu.get_barrier_semaphore()

    def greet(i, carry):
        d = lax.rem(me + i, devices)
        pl.semaphore_signal(
            barrier, inc=1, device_id=(lax.div(d, grp_count), lax.rem(d, grp_count)), device_id_type=MESH
        )
        return carry

    lax.fori_loop(1, devices, greet, 0)

    def stage(i, p):
        c = far_first(i, chans, t, tm_count)
        staged[c, p] = raw[c, p].astype(f32).reshape(2, rows, f).astype(bf16)

    def stage_early(i, carry):
        stage(i, 0)
        return carry

    early = chans // 3
    fetch.wait()
    lax.fori_loop(0, early, stage_early, 0)
    pl.semaphore_wait(barrier, devices - 1)

    k_slot = pl.ds(pl.multiple_of(t * k_rows, k_rows), k_rows)
    z_slot = pl.ds(pl.multiple_of(me * rows, rows), rows)

    def chirp_copy(i):
        return pltpu.make_async_remote_copy(
            src_ref=rows16.at[i], dst_ref=phase.at[k_slot], send_sem=chirp_send.at[i],
            recv_sem=chirp_recv, device_id=(i, j), device_id_type=MESH,
        )

    def volt_copy(c, p, ot, oj):
        return pltpu.make_async_remote_copy(
            src_ref=staged.at[c, p], dst_ref=z.at[p, :, z_slot], send_sem=volt_send.at[p, c],
            recv_sem=volt_recv.at[p], device_id=(ot, oj), device_id_type=MESH,
        )

    def over_channels(act):
        def step(i, carry):
            c = far_first(i, chans, t, tm_count)
            ot, oj = owner_of(c)
            act(i, c, ot, oj)
            return carry

        lax.fori_loop(0, chans, step, 0)

    def elsewhere(ot, oj):
        return (oj != j) | (ot != t)

    def send_first(i, c, ot, oj):
        @pl.when(elsewhere(ot, oj))
        def _():
            volt_copy(c, 0, ot, oj).start()

        @pl.when(i + early < chans)
        def _():
            stage(i + early, 0)

    over_channels(send_first)

    def own(p):
        @pl.when(active)
        def _():
            pltpu.make_async_copy(staged.at[mine, p], z.at[p, :, z_slot], volt_recv.at[p]).start()

    own(0)

    def send_rows(i, c):
        load_rows(i, c).wait()
        rows16[i] = jnp.round(rows32[i] * (32768.0 / math.pi)).astype(jnp.int32).astype(jnp.int16)

        @pl.when(i != t)
        def _():
            chirp_copy(i).start()

        @pl.when(i == t)
        def _():
            pltpu.make_async_copy(rows16.at[i], phase.at[k_slot], chirp_recv).start()

    over_column(send_rows)

    for p in range(1, pols):
        def stage_next(i, carry):
            stage(i, p)
            return carry

        lax.fori_loop(0, chans, stage_next, 0)
        own(p)

        def send_next(i, c, ot, oj):
            @pl.when(elsewhere(ot, oj))
            def _():
                volt_copy(c, p - 1, ot, oj).wait_send()
                volt_copy(c, p, ot, oj).start()

        over_channels(send_next)

    for load in loads:
        load.wait()

    def power_copy(d):
        return pltpu.make_async_remote_copy(
            src_ref=power.at[d],
            dst_ref=gathered.at[mine], send_sem=power_send.at[d], recv_sem=power_recv,
            device_id=(lax.div(d, grp_count), lax.rem(d, grp_count)), device_id_type=MESH,
        )

    @pl.when(active)
    def _():
        pltpu.make_async_copy(phase, phase, chirp_recv).wait()

        def chirp_step(i, carry):
            part = pl.ds(pl.multiple_of(i * 64, 64), 64)
            cc[part], cs[part] = turn_tables(shifts[mine], phase[part], order[...], i * 64)
            return carry

        lax.fori_loop(0, f // 64, chirp_step, 0)
        summed[...] = jnp.zeros_like(summed)

        def pol_step(p, carry):
            pltpu.make_async_copy(z.at[p], z.at[p], volt_recv.at[p]).wait()

            def step(i, inner):
                samples = z[p].reshape(2 * f, f)
                rows_step(i, samples, left, ahead, back, turned, cc, cs, v, tile)
                return inner

            lax.fori_loop(0, f // tile, step, 0)
            last_step(last, v, summed)
            return carry

        lax.fori_loop(0, pols, pol_step, 0)

        q = t_rows // 2
        for d in range(devices):
            for odd in (0, 1):
                power[d, odd * q : (odd + 1) * q] = summed[odd, d * q : (d + 1) * q]

        def send_power(i, carry):
            d = far_first(i, devices, t, tm_count, j)

            @pl.when(d != me)
            def _():
                power_copy(d).start()

            return carry

        lax.fori_loop(0, devices, send_power, 0)
        pltpu.make_async_copy(power.at[me], gathered.at[mine], power_recv).start()

    pltpu.make_async_copy(gathered, gathered, power_recv).wait()
    for g in range(out.shape[0]):
        total = jnp.zeros((t_rows, f), f32)
        count = jnp.int32(0)
        for c in range(chans):
            member = (group_of[c] == g).astype(jnp.int32)
            count = count + member
            total = total + member.astype(f32) * gathered[c]
        total = total / jnp.full((t_rows, f), 2 * count, jnp.int32).astype(f32)
        for r in range(t_rows):
            when = 2 * r if r < t_rows // 2 else 2 * r - t_rows + 1
            out[g : g + 1, when * f : (when + 1) * f] = total[r : r + 1]

    def wait_rows(i, c):
        @pl.when(i != t)
        def _():
            chirp_copy(i).wait_send()

    def wait_volt(i, c, ot, oj):
        @pl.when(elsewhere(ot, oj))
        def _():
            volt_copy(c, pols - 1, ot, oj).wait_send()

    over_column(wait_rows)
    over_channels(wait_volt)

    @pl.when(active)
    def _():
        def wait_power(i, carry):
            power_copy(lax.rem(me + i, devices)).wait_send()
            return carry

        lax.fori_loop(1, devices, wait_power, 0)


def fused(shifts, group_of, volt, chirp, tm_count, grp_count, groups):
    chans, pols, _, local_len = volt.shape
    f = chirp.shape[2]
    rows = local_len // f
    devices = tm_count * grp_count
    t_rows = f // 2 // devices
    smem = pl.BlockSpec(memory_space=pltpu.SMEM)
    hbm = pl.BlockSpec(memory_space=pl.ANY)
    dma = pltpu.SemaphoreType.DMA
    square = lambda kind: pltpu.VMEM((f, f), kind)
    return pl.pallas_call(
        functools.partial(fused_kernel, tm_count=tm_count, grp_count=grp_count, tile=f // 2),
        out_shape=jax.ShapeDtypeStruct((groups, t_rows * f), f32),
        in_specs=[smem, smem] + [hbm] * 8,
        out_specs=pl.BlockSpec(memory_space=pltpu.VMEM),
        scratch_shapes=[
            pltpu.VMEM(volt.shape, bf16),
            pltpu.VMEM((chans, pols, 2, rows, f), bf16),
            pltpu.VMEM((tm_count, chirp.shape[1], f), f32),
            pltpu.VMEM((tm_count, chirp.shape[1], f), jnp.int16),
            pltpu.VMEM((pols, 2, f, f), bf16),
            square(jnp.int16),
            pltpu.VMEM((chans, t_rows, f), f32),
            pltpu.VMEM((2, f // 4, f), f32),
            pltpu.VMEM((devices, t_rows, f), f32),
            *[pltpu.VMEM(t.shape, t.dtype) for t in tables(f)],
            square(f32),
            square(f32),
            pltpu.VMEM((2 * f, f), f32),
            dma,
            dma((6,)),
            dma((tm_count,)),
            dma((pols, chans)),
            dma((pols,)),
            dma((tm_count,)),
            dma,
            dma((devices,)),
            dma,
        ],
        compiler_params=pltpu.CompilerParams(
            vmem_limit_bytes=56 * 1024 * 1024, collective_id=0, has_side_effects=True
        ),
    )(shifts, group_of, volt, chirp, *(jnp.asarray(t) for t in tables(f)))


def on_device(voltages, chirp_phase, intersection, group_of):
    tm_count = lax.axis_size("tm")
    grp_count = lax.axis_size("grp")
    devices = tm_count * grp_count
    tm_rank = lax.axis_index("tm")
    grp_rank = lax.axis_index("grp")
    me = tm_rank * grp_count + grp_rank
    beams, chans, pols, _, local_len = voltages.shape
    f = chirp_phase.shape[2]
    rows = local_len // f
    groups = 4
    member = (group_of[None, :] == jnp.arange(groups, dtype=jnp.int32)[:, None]).astype(f32)
    shares = member / (2.0 * jnp.sum(member, axis=1, keepdims=True))
    whole_tiles = rows % 16 == 0 and chirp_phase.shape[1] % 16 == 0 and (f // 2) % (8 * devices) == 0
    if staggered(chans, tm_count, grp_count) and whole_tiles and f * f % 65536 == 0:
        result = fused(
            intersection,
            group_of,
            voltages[0],
            chirp_phase,
            tm_count,
            grp_count,
            groups,
        )
        return result.reshape(beams, groups, -1)
    owners = np.arange(chans) * devices // chans
    owned = np.zeros(devices, np.int32)
    owned[owners] = np.arange(chans)
    active = np.zeros(devices, np.float32)
    active[owners] = 1.0
    mine = jnp.asarray(owned)[me]
    out = jnp.take(voltages[0], owned, axis=0)
    got = lax.all_to_all(out, ("tm", "grp"), split_axis=0, concat_axis=0, tiled=True)
    z = jnp.transpose(got.reshape(devices, pols, 2, rows, f), (1, 2, 0, 3, 4)).reshape(pols, 2 * f, f)
    column = jnp.asarray(owned.reshape(tm_count, grp_count))[:, grp_rank]
    phase = lax.all_to_all(
        jnp.take(chirp_phase, column, axis=0), "tm", split_axis=0, concat_axis=0, tiled=True
    ).reshape(f, f)
    power = channel_power(intersection[mine][None], z, phase)
    moved = lax.all_to_all(
        power.reshape(devices, -1), ("tm", "grp"), split_axis=0, concat_axis=0, tiled=True
    )
    weights = jnp.take(shares, owned, axis=1) * active[None, :]
    result = jnp.sum(weights[:, :, None] * moved[None], axis=1)
    return result[None]


def solution(mesh):
    in_specs = (P(None, None, None, None, ("tm", "grp")), P(None, "tm", None), P(), P())
    out_specs = P(None, None, ("tm", "grp"))
    return jax.shard_map(
        on_device, mesh=mesh, in_specs=in_specs, out_specs=out_specs, check_vma=False
    )
```

```python
import functools
import math

import jax
import jax.numpy as jnp
import numpy as np
from jax import lax
from jax.experimental import pallas as pl
from jax.experimental.pallas import tpu as pltpu
from jax.sharding import PartitionSpec as P

f32 = jnp.float32
bf16 = jnp.bfloat16


def split(values):
    high = values.astype(bf16)
    return high, (values - high.astype(f32)).astype(bf16)


def np_split(values):
    high = values.astype(np.float32).astype(bf16)
    low = (values - high.astype(np.float64)).astype(np.float32).astype(bf16)
    return np.asarray(high), np.asarray(low)


def halves(c, s, sign):
    return np.block([[c, sign * s], [-sign * s, c]])


@functools.lru_cache(None)
def tables(f):
    h = f // 2
    index = np.arange(f)
    product = index[:, None] * index[None, :]
    angle = 2.0 * np.pi * (product % f) / f
    c, s = np.cos(angle), np.sin(angle)
    left = np.stack(np_split(np.block([[c, s], [-s, c]])))
    ahead, back, last = [], [], []
    for odd in (0, 1):
        ahead.append(np.stack(np_split(halves(c[:h, odd::2], s[:h, odd::2], -1))))
        back.append(np.stack(np_split(halves(c[odd::2, :h], s[odd::2, :h], 1))))
        part = slice(odd, h, 2)
        last.append(np.stack(np_split(np.block([[c[part, :h], -s[part, :h]], [s[part, :h], c[part, :h]]]))))
    twist = 2.0 * np.pi * product / (f * f)
    turned = np.stack([np.cos(twist), np.sin(twist)]).astype(np.float32)
    order = np.eye(f)[:, np.concatenate([index[::2], index[1::2]])].astype(bf16)
    return left, np.stack(ahead), np.stack(back), np.stack(last), turned, np.asarray(order)


def column_ids(shape):
    h = shape[1] // 2
    cols = lax.broadcasted_iota(jnp.int32, shape, 1)
    return 2 * (cols & (h - 1)) + (cols >= h).astype(jnp.int32)


@functools.lru_cache(None)
def turn_polynomials():
    nodes = 0.125 + 0.13 * np.cos(np.pi * (np.arange(200) + 0.5) / 200)
    root = np.sqrt(np.abs(nodes))
    fits = []
    for values, degree in (
        (np.cos(2 * np.pi * root), 8),
        (np.sin(2 * np.pi * root) / root, 8),
    ):
        keep = nodes > 0
        fit = np.polynomial.Chebyshev.fit(nodes[keep], values[keep], degree, domain=[0, 0.25])
        fits.append([float(x) for x in fit.convert(kind=np.polynomial.Polynomial).coef])
    return fits


def horner(q, coefficients):
    total = jnp.full_like(q, coefficients[-1])
    for x in coefficients[-2::-1]:
        total = total * q + x
    return total


def chirp_tables(shift, phase, k1):
    f = phase.shape[1]
    nfft = f * f
    rows = k1 + lax.broadcasted_iota(jnp.int32, phase.shape, 0)
    cols = column_ids(phase.shape)
    ramp = (rows * shift + f * ((cols * shift) & (f - 1))) & (nfft - 1)
    turns = phase * (0.5 / math.pi) + ramp.astype(f32) * (1.0 / nfft)
    rest = turns - jnp.round(turns)
    q = rest * rest
    cos_fit, sin_fit = turn_polynomials()
    scale = 1.0 / nfft
    return horner(q, cos_fit) * scale, horner(q, sin_fit) * (rest * scale)


def turn_tables(shift, fraction, order, k1):
    whole = fraction.astype(jnp.int32)
    upper = whole >> 8
    parts = jnp.concatenate([upper, whole - upper * 256], axis=0).astype(f32).astype(bf16)
    moved = mm(parts, order).astype(jnp.int32)
    fraction = moved[: whole.shape[0]] * 256 + moved[whole.shape[0] :]
    f = fraction.shape[1]
    nfft = f * f
    rows = k1 + lax.broadcasted_iota(jnp.int32, fraction.shape, 0)
    cols = column_ids(fraction.shape)
    ramp = rows * shift + f * ((cols * shift) & (f - 1))
    steps = fraction * (nfft // 65536) + ramp
    rest = (((steps + nfft // 2) & (nfft - 1)) - nfft // 2).astype(f32) * (1.0 / nfft)
    q = rest * rest
    cos_fit, sin_fit = turn_polynomials()
    scale = 1.0 / nfft
    return horner(q, cos_fit) * scale, horner(q, sin_fit) * (rest * scale)


def mm(a, b):
    return jnp.dot(a, b, preferred_element_type=f32)


def three(values, high, low):
    rows = values.shape[0]
    vh, vl = split(values)
    both = mm(jnp.concatenate([vh, vl], axis=0), high)
    return both[:rows] + both[rows:] + mm(vh, low)


def rows_step(i, z, left, ahead, back, turned, cc, cs, v, tile):
    f = cc.shape[0]
    h = f // 2
    top = pl.ds(pl.multiple_of(i * tile, tile), tile)
    bot = pl.ds(pl.multiple_of(f + i * tile, tile), tile)
    lhs = jnp.concatenate([left[0, top], left[0, bot], left[1, top], left[1, bot]], axis=0)
    r = mm(lhs, z)
    yr = r[:tile] + r[2 * tile : 3 * tile]
    yi = r[tile : 2 * tile] + r[3 * tile :]
    c, s = turned[0, top], turned[1, top]
    ar, ai = yr * c + yi * s, yi * c - yr * s
    found = []
    for odd in (0, 1):
        sign = 1 - 2 * odd
        pair = [ar[:, :h] + sign * ar[:, h:], ai[:, :h] + sign * ai[:, h:]]
        spec = three(jnp.concatenate(pair, axis=1), ahead[odd, 0], ahead[odd, 1])
        zr, zi = spec[:, :h], spec[:, h:]
        cols = slice(odd * h, (odd + 1) * h)
        hc, hs = cc[top, cols], cs[top, cols]
        pair = [zr * hc - zi * hs, zr * hs + zi * hc]
        found.append(three(jnp.concatenate(pair, axis=1), back[odd, 0], back[odd, 1]))
    plus, minus = found[0] + found[1], found[0] - found[1]
    vr = jnp.concatenate([plus[:, :h], minus[:, :h]], axis=1)
    vi = jnp.concatenate([plus[:, h:], minus[:, h:]], axis=1)
    v[top] = vr * c - vi * s
    v[bot] = vr * s + vi * c


def last_step(last, v, power):
    f = v.shape[1]
    h, q = f // 2, f // 4
    for odd in (0, 1):
        sign = 1 - 2 * odd
        both = [v[:h] + sign * v[h:f], v[f : f + h] + sign * v[f + h :]]
        vh, vl = split(jnp.concatenate(both, axis=0))
        high, low = last[odd, 0], last[odd, 1]
        r = mm(jnp.concatenate([high, low], axis=0), vh)
        sig = r[:h] + r[h:] + mm(high, vl)
        sr, si = sig[:q], sig[q:]
        power[odd] += sr * sr + si * si


def local_kernel(shift, z, phase, left, ahead, back, last, turned, order, power, cc, cs, v, *, tile):
    f = phase.shape[0]
    pols = z.shape[0]

    def chirp_step(i, carry):
        rows = pl.ds(pl.multiple_of(i * 64, 64), 64)
        cc[rows], cs[rows] = chirp_tables(shift[0], phase[rows], i * 64)
        return carry

    lax.fori_loop(0, f // 64, chirp_step, 0)
    power[...] = jnp.zeros_like(power)

    def pol_step(p, carry):
        def step(i, inner):
            rows_step(i, z[p], left, ahead, back, turned, cc, cs, v, tile)
            return inner

        lax.fori_loop(0, f // tile, step, 0)
        last_step(last, v, power)
        return carry

    lax.fori_loop(0, pols, pol_step, 0)


def channel_power(shift, z, phase):
    f = phase.shape[0]
    tile = f // 2
    smem = pl.BlockSpec(memory_space=pltpu.SMEM)
    vmem = pl.BlockSpec(memory_space=pltpu.VMEM)
    phase = jnp.concatenate([phase[:, ::2], phase[:, 1::2]], axis=1)
    power = pl.pallas_call(
        functools.partial(local_kernel, tile=tile),
        out_shape=jax.ShapeDtypeStruct((2, f // 4, f), f32),
        in_specs=[smem] + [vmem] * 8,
        out_specs=vmem,
        scratch_shapes=[
            pltpu.VMEM((f, f), f32),
            pltpu.VMEM((f, f), f32),
            pltpu.VMEM((2 * f, f), f32),
        ],
        compiler_params=pltpu.CompilerParams(vmem_limit_bytes=56 * 1024 * 1024),
    )(shift, z, phase, *(jnp.asarray(t) for t in tables(f)))
    return jnp.swapaxes(power, 0, 1).reshape(f // 2, f)


MESH = pl.DeviceIdType.MESH


def staggered(chans, tm_count, grp_count):
    return grp_count == 4 and chans == tm_count * (grp_count - 1)


def owner_of(c):
    t, k = lax.div(c, 3), lax.rem(c, 3)
    a = lax.rem(lax.div(t, 2) + lax.rem(t, 2), 2)
    return t, k + a * lax.div(k + 1, 2)


def channel_at(t, j):
    a = lax.rem(lax.div(t, 2) + lax.rem(t, 2), 2)
    return 3 * t + j - a * lax.div(j + 3, 4), j != 3 - 2 * a


def fused_kernel(
    shifts, group_of, volt, chirp, h_left, h_ahead, h_back, h_last, h_turned, h_order, out,
    raw, staged, rows32, rows16, z, phase, gathered, summed, power, left, ahead, back, last, turned, order, cc, cs, v,
    raw_sem, table_sem, rows_sem, volt_send, volt_recv, chirp_send, chirp_recv, power_send, power_recv,
    *, tm_count, grp_count, tile,
):
    t, j = lax.axis_index("tm"), lax.axis_index("grp")
    devices = tm_count * grp_count
    me = t * grp_count + j
    chans, pols, _, rows, f = staged.shape
    k_rows = chirp.shape[1]
    t_rows = gathered.shape[1]
    mine, active = channel_at(t, j)

    first = 3 * t
    fetch = pltpu.make_async_copy(volt, raw, raw_sem)
    fetch.start()
    pairs = [(h_left, left), (h_ahead, ahead), (h_back, back)]
    pairs += [(h_last, last), (h_turned, turned), (h_order, order)]
    loads = [pltpu.make_async_copy(a, b, table_sem.at[i]) for i, (a, b) in enumerate(pairs)]
    for load in loads:
        load.start()

    def over_column(act):
        def step(i, carry):
            c, owned = channel_at(i, j)

            @pl.when(owned)
            def _():
                act(i, c)

            return carry

        lax.fori_loop(0, tm_count, step, 0)

    def load_rows(i, c):
        return pltpu.make_async_copy(chirp.at[c], rows32.at[i], rows_sem.at[i])

    over_column(lambda i, c: load_rows(i, c).start())
    barrier = pltpu.get_barrier_semaphore()

    def greet(i, carry):
        d = lax.rem(me + i, devices)
        pl.semaphore_signal(
            barrier, inc=1, device_id=(lax.div(d, grp_count), lax.rem(d, grp_count)), device_id_type=MESH
        )
        return carry

    lax.fori_loop(1, devices, greet, 0)

    def stage(i, p):
        c = lax.rem(first + i, chans)
        staged[c, p] = raw[c, p].astype(f32).reshape(2, rows, f).astype(bf16)

    def code_rows(i, c):
        load_rows(i, c).wait()
        rows16[i] = jnp.round(rows32[i] * (32768.0 / math.pi)).astype(jnp.int32).astype(jnp.int16)

    over_column(code_rows)
    pl.semaphore_wait(barrier, devices - 1)

    k_slot = pl.ds(pl.multiple_of(t * k_rows, k_rows), k_rows)
    z_slot = pl.ds(pl.multiple_of(me * rows, rows), rows)

    def chirp_copy(i):
        return pltpu.make_async_remote_copy(
            src_ref=rows16.at[i], dst_ref=phase.at[k_slot], send_sem=chirp_send.at[i],
            recv_sem=chirp_recv, device_id=(i, j), device_id_type=MESH,
        )

    def volt_copy(c, p, ot, oj):
        return pltpu.make_async_remote_copy(
            src_ref=staged.at[c, p], dst_ref=z.at[p, :, z_slot], send_sem=volt_send.at[p, c],
            recv_sem=volt_recv.at[p], device_id=(ot, oj), device_id_type=MESH,
        )

    def over_channels(start, act):
        def step(i, carry):
            c = lax.rem(start + i, chans)
            ot, oj = owner_of(c)
            act(i, c, ot, oj)
            return carry

        lax.fori_loop(0, chans, step, 0)

    def elsewhere(ot, oj):
        return (oj != j) | (ot != t)

    def send_rows(i, c):
        @pl.when(i != t)
        def _():
            chirp_copy(i).start()

        @pl.when(i == t)
        def _():
            pltpu.make_async_copy(rows16.at[i], phase.at[k_slot], chirp_recv).start()

    over_column(send_rows)

    fetch.wait()

    def send_first(i, c, ot, oj):
        stage(i, 0)

        @pl.when(elsewhere(ot, oj))
        def _():
            volt_copy(c, 0, ot, oj).start()

    over_channels(first, send_first)

    def own(p):
        @pl.when(active)
        def _():
            pltpu.make_async_copy(staged.at[mine, p], z.at[p, :, z_slot], volt_recv.at[p]).start()

    own(0)

    for p in range(1, pols):
        def stage_next(i, carry):
            stage(i, p)
            return carry

        lax.fori_loop(0, chans, stage_next, 0)
        own(p)

        def send_next(i, c, ot, oj):
            @pl.when(elsewhere(ot, oj))
            def _():
                volt_copy(c, p - 1, ot, oj).wait_send()
                volt_copy(c, p, ot, oj).start()

        over_channels(first, send_next)

    for load in loads:
        load.wait()

    def power_copy(d):
        return pltpu.make_async_remote_copy(
            src_ref=power.at[d],
            dst_ref=gathered.at[mine], send_sem=power_send.at[d], recv_sem=power_recv,
            device_id=(lax.div(d, grp_count), lax.rem(d, grp_count)), device_id_type=MESH,
        )

    @pl.when(active)
    def _():
        pltpu.make_async_copy(phase, phase, chirp_recv).wait()

        def chirp_step(i, carry):
            part = pl.ds(pl.multiple_of(i * 64, 64), 64)
            cc[part], cs[part] = turn_tables(shifts[mine], phase[part], order[...], i * 64)
            return carry

        lax.fori_loop(0, f // 64, chirp_step, 0)
        summed[...] = jnp.zeros_like(summed)

        def pol_step(p, carry):
            pltpu.make_async_copy(z.at[p], z.at[p], volt_recv.at[p]).wait()

            def step(i, inner):
                samples = z[p].reshape(2 * f, f)
                rows_step(i, samples, left, ahead, back, turned, cc, cs, v, tile)
                return inner

            lax.fori_loop(0, f // tile, step, 0)
            last_step(last, v, summed)
            return carry

        lax.fori_loop(0, pols, pol_step, 0)

        q = t_rows // 2
        for d in range(devices):
            for odd in (0, 1):
                power[d, odd * q : (odd + 1) * q] = summed[odd, d * q : (d + 1) * q]

        def send_power(i, carry):
            power_copy(lax.rem(me + i, devices)).start()
            return carry

        lax.fori_loop(1, devices, send_power, 0)
        pltpu.make_async_copy(power.at[me], gathered.at[mine], power_recv).start()

    pltpu.make_async_copy(gathered, gathered, power_recv).wait()
    for g in range(out.shape[0]):
        total = jnp.zeros((t_rows, f), f32)
        count = jnp.int32(0)
        for c in range(chans):
            member = (group_of[c] == g).astype(jnp.int32)
            count = count + member
            total = total + member.astype(f32) * gathered[c]
        total = total / jnp.full((t_rows, f), 2 * count, jnp.int32).astype(f32)
        for r in range(t_rows):
            when = 2 * r if r < t_rows // 2 else 2 * r - t_rows + 1
            out[g : g + 1, when * f : (when + 1) * f] = total[r : r + 1]

    def wait_rows(i, c):
        @pl.when(i != t)
        def _():
            chirp_copy(i).wait_send()

    def wait_volt(i, c, ot, oj):
        @pl.when(elsewhere(ot, oj))
        def _():
            volt_copy(c, pols - 1, ot, oj).wait_send()

    over_column(wait_rows)
    over_channels(first, wait_volt)

    @pl.when(active)
    def _():
        def wait_power(i, carry):
            power_copy(lax.rem(me + i, devices)).wait_send()
            return carry

        lax.fori_loop(1, devices, wait_power, 0)


def fused(shifts, group_of, volt, chirp, tm_count, grp_count, groups):
    chans, pols, _, local_len = volt.shape
    f = chirp.shape[2]
    rows = local_len // f
    devices = tm_count * grp_count
    t_rows = f // 2 // devices
    smem = pl.BlockSpec(memory_space=pltpu.SMEM)
    hbm = pl.BlockSpec(memory_space=pl.ANY)
    dma = pltpu.SemaphoreType.DMA
    square = lambda kind: pltpu.VMEM((f, f), kind)
    return pl.pallas_call(
        functools.partial(fused_kernel, tm_count=tm_count, grp_count=grp_count, tile=f // 2),
        out_shape=jax.ShapeDtypeStruct((groups, t_rows * f), f32),
        in_specs=[smem, smem] + [hbm] * 8,
        out_specs=pl.BlockSpec(memory_space=pltpu.VMEM),
        scratch_shapes=[
            pltpu.VMEM(volt.shape, bf16),
            pltpu.VMEM((chans, pols, 2, rows, f), bf16),
            pltpu.VMEM((tm_count, chirp.shape[1], f), f32),
            pltpu.VMEM((tm_count, chirp.shape[1], f), jnp.int16),
            pltpu.VMEM((pols, 2, f, f), bf16),
            square(jnp.int16),
            pltpu.VMEM((chans, t_rows, f), f32),
            pltpu.VMEM((2, f // 4, f), f32),
            pltpu.VMEM((devices, t_rows, f), f32),
            *[pltpu.VMEM(t.shape, t.dtype) for t in tables(f)],
            square(f32),
            square(f32),
            pltpu.VMEM((2 * f, f), f32),
            dma,
            dma((6,)),
            dma((tm_count,)),
            dma((pols, chans)),
            dma((pols,)),
            dma((tm_count,)),
            dma,
            dma((devices,)),
            dma,
        ],
        compiler_params=pltpu.CompilerParams(
            vmem_limit_bytes=56 * 1024 * 1024, collective_id=0, has_side_effects=True
        ),
    )(shifts, group_of, volt, chirp, *(jnp.asarray(t) for t in tables(f)))


def on_device(voltages, chirp_phase, intersection, group_of):
    tm_count = lax.axis_size("tm")
    grp_count = lax.axis_size("grp")
    devices = tm_count * grp_count
    tm_rank = lax.axis_index("tm")
    grp_rank = lax.axis_index("grp")
    me = tm_rank * grp_count + grp_rank
    beams, chans, pols, _, local_len = voltages.shape
    f = chirp_phase.shape[2]
    rows = local_len // f
    groups = 4
    member = (group_of[None, :] == jnp.arange(groups, dtype=jnp.int32)[:, None]).astype(f32)
    shares = member / (2.0 * jnp.sum(member, axis=1, keepdims=True))
    whole_tiles = rows % 16 == 0 and chirp_phase.shape[1] % 16 == 0 and (f // 2) % (8 * devices) == 0
    if staggered(chans, tm_count, grp_count) and whole_tiles and f * f % 65536 == 0:
        result = fused(
            intersection,
            group_of,
            voltages[0],
            chirp_phase,
            tm_count,
            grp_count,
            groups,
        )
        return result.reshape(beams, groups, -1)
    owners = np.arange(chans) * devices // chans
    owned = np.zeros(devices, np.int32)
    owned[owners] = np.arange(chans)
    active = np.zeros(devices, np.float32)
    active[owners] = 1.0
    mine = jnp.asarray(owned)[me]
    out = jnp.take(voltages[0], owned, axis=0)
    got = lax.all_to_all(out, ("tm", "grp"), split_axis=0, concat_axis=0, tiled=True)
    z = jnp.transpose(got.reshape(devices, pols, 2, rows, f), (1, 2, 0, 3, 4)).reshape(pols, 2 * f, f)
    column = jnp.asarray(owned.reshape(tm_count, grp_count))[:, grp_rank]
    phase = lax.all_to_all(
        jnp.take(chirp_phase, column, axis=0), "tm", split_axis=0, concat_axis=0, tiled=True
    ).reshape(f, f)
    power = channel_power(intersection[mine][None], z, phase)
    moved = lax.all_to_all(
        power.reshape(devices, -1), ("tm", "grp"), split_axis=0, concat_axis=0, tiled=True
    )
    weights = jnp.take(shares, owned, axis=1) * active[None, :]
    result = jnp.sum(weights[:, :, None] * moved[None], axis=1)
    return result[None]


def solution(mesh):
    in_specs = (P(None, None, None, None, ("tm", "grp")), P(None, "tm", None), P(), P())
    out_specs = P(None, None, ("tm", "grp"))
    return jax.shard_map(
        on_device, mesh=mesh, in_specs=in_specs, out_specs=out_specs, check_vma=False
    )
```
